32 devices in a mesh: batch: 16 (over z, y, x), hid: 2 (over core).
Axes of the slice: x: 2, y: 2, z: 4, core: 2. Of those that a mesh axis runs over, the one named last changes fastest.
Arguments:
- raw_maps: bfloat16 [64, 24, 24, 512], P(('batch', 'hid')), may hold values from -32 to 32
- partner: int32 [64], P(('batch', 'hid')), may hold values from 0 to 63, as said below
- ratios: float32 [64], P(('batch', 'hid')), may hold values from 0.3 to 0.7
- offsets: int32 [64, 2], P(('batch', 'hid')), may hold values from 0 to 10
- flip_bits: int32 [64], P(('batch', 'hid')), may hold values 0 or 1
- size_class: int32 [64], P(('batch', 'hid')), may hold values 0 or 1
- proj_in: bfloat16 [512, 512], P(('batch', 'hid')), may hold values from -0.25 to 0.25
- kernel_large: bfloat16 [27, 27, 512], P(None, None, ('batch', 'hid')), may hold values from -0.21875 to 0.21875
- kernel_small: bfloat16 [5, 5, 512], P(None, None, ('batch', 'hid')), may hold values from -1.25 to 1.25
- proj_out: bfloat16 [512, 512], P(('batch', 'hid')), may hold values from -0.25 to 0.25
- norm_gain: bfloat16 [5, 512], P(None, ('batch', 'hid')), may hold values from 0.099609375 to 1.8984375
- norm_bias: bfloat16 [5, 512], P(None, ('batch', 'hid')), may hold values from -2 to 2
- ffn_up: bfloat16 [512, 2048], P('batch', 'hid'), may hold values from -0.25 to 0.25
- ffn_down: bfloat16 [2048, 512], P('hid', 'batch'), may hold values from -0.125 to 0.125
- cotangent: bfloat16 [64, 24, 24, 512], P(('batch', 'hid')), may hold values from -6 to 6
Outputs:
- output: bfloat16 [64, 24, 24, 512], P(('batch', 'hid'))
- grad_raw_maps: float32 [64, 24, 24, 512], P(('batch', 'hid'))
- grad_proj_in: float32 [512, 512], P(('batch', 'hid'))
- grad_kernel_large: float32 [27, 27, 512], P(None, None, ('batch', 'hid'))
- grad_kernel_small: float32 [5, 5, 512], P(None, None, ('batch', 'hid'))
- grad_proj_out: float32 [512, 512], P(('batch', 'hid'))
- grad_norm_gain: float32 [5, 512], P(None, ('batch', 'hid'))
- grad_norm_bias: float32 [5, 512], P(None, ('batch', 'hid'))
- grad_ffn_up: float32 [512, 2048], P('batch', 'hid')
- grad_ffn_down: float32 [2048, 512], P('hid', 'batch')
The draws below stay inside these ranges and needn't reach their ends.
Inputs may be any that keep to these rules, and one draw needn't show every extreme that they name: partner[i] lies among the images from 2 * (i // 2) - 2 to 2 * (i // 2) + 1, taken modulo 64; where i is a multiple of 2 it lies among the first 2 of these.
All inputs are finite; a program needn't handle non-finite values. No bound on the sum of `flip_bits` or of `size_class` on one device may be relied on, other than what follows from the above.
Results may differ from the reference program's by a relative error of at most 0.02.
Values may be sent and summed in bfloat16 or wider, within the bound.
No kernel may reach another device: no remote copies, remote signals or barrier semaphores. Data moves between devices by JAX's collectives and lax.ppermute only.
A program may use at most 192 MiB of HBM per device.

```python
import jax
import jax.numpy as jnp
import numpy as np
from jax import lax

C = 512
FF = 2048
KL = 27
KS = 5
CANVAS = 24
SMALL = 14
IMG_DEV = 2
IMAGES = 64


def draw_raw_maps(key, part):
    key = jax.random.fold_in(key, 11)
    keys = jax.random.split(key, 3)
    image_scale = jnp.exp(jax.random.uniform(keys[0], (IMAGES,), jnp.float32, jnp.log(0.6), jnp.log(1.2)))
    channel_scale = jnp.exp(jax.random.uniform(keys[1], (C,), jnp.float32, jnp.log(0.3), jnp.log(3.0)))
    owner = (jnp.arange(IMAGES) // IMG_DEV).astype(jnp.float32)
    last_owner = max(IMAGES // IMG_DEV - 1, 1)
    rising = 3.0 ** (owner / last_owner) / 1.7
    noise = jax.random.normal(keys[2], (IMAGES, CANVAS, CANVAS, C), jnp.float32)
    values = noise * (image_scale * rising)[:, None, None, None] * channel_scale
    return jnp.clip(values, -32.0, 32.0).astype(jnp.bfloat16)


def draw_partner(key, part):
    key = jax.random.fold_in(key, 23)
    first_key, other_key = jax.random.split(key)
    image_id = jnp.arange(IMAGES, dtype=jnp.int32)
    owner_first = image_id // IMG_DEV * IMG_DEV
    anywhere = jax.random.randint(other_key, (IMAGES,), -IMG_DEV, IMG_DEV, dtype=jnp.int32)
    earlier = jax.random.randint(first_key, (IMAGES,), -IMG_DEV, 0, dtype=jnp.int32)
    step_back = jnp.where(image_id % IMG_DEV == 0, earlier, anywhere)
    return jnp.mod(owner_first + step_back, IMAGES).astype(jnp.int32)


def set_ends(drawn, own_key, smallest, largest):
    place = [jax.random.randint(jax.random.fold_in(own_key, axis), (), 0, length) for axis, length in enumerate(drawn.shape)]
    main_axis = drawn.shape.index(max(drawn.shape))
    next_to = place[:main_axis] + [(place[main_axis] + 1) % drawn.shape[main_axis]] + place[main_axis + 1:]
    return drawn.at[tuple(place)].set(smallest).at[tuple(next_to)].set(largest)


def levels(stream_key, shape, pieces, smallest, top_value):
    def one(dim, shards_of):
        steps = jax.random.uniform(jax.random.fold_in(jax.random.fold_in(stream_key, 6), dim), (shards_of,), jnp.float32, smallest / len(pieces), top_value / len(pieces))
        return jnp.repeat(jnp.exp(steps), shape[dim] // shards_of).reshape((-1,) + (1,) * (len(shape) - dim - 1))

    loudness = one(*pieces[0])
    for cut in pieces[1:]:
        loudness = loudness * one(*cut)
    return loudness


def bell_draw(rng, shape, deviation, reach, cuts=(), kind=jnp.bfloat16):
    array = jax.random.normal(rng, shape, jnp.float32) * deviation
    if len(cuts) > 0:
        array = levels(rng, shape, cuts, -0.22, 0.18) * array
    return jnp.clip(array, min=-reach, max=reach).astype(kind)


def setup_inputs(seed: int = 0) -> dict:
    arg_keys = jax.random.split(jax.random.key(seed), 16)
    return {
        "raw_maps": draw_raw_maps(jax.random.fold_in(arg_keys[15], 71), 0),
        "partner": draw_partner(jax.random.fold_in(arg_keys[15], 71), 0),
        "ratios": jnp.clip(0.3 + 0.39999998 * jax.random.uniform(arg_keys[2], (IMAGES,), jnp.float32) ** levels(arg_keys[2], (IMAGES,), ((0, 32),), -0.2, 0.2), 0.3, 0.7),
        "offsets": set_ends(jax.random.randint(arg_keys[3], (IMAGES, 2), 0, CANVAS - SMALL + 1), jax.random.fold_in(arg_keys[3], 1), 0, CANVAS - SMALL).astype(jnp.int32),
        "flip_bits": set_ends((jax.random.randint(arg_keys[4], (IMAGES,), 0, 2) < 1).astype(jnp.int32), jax.random.fold_in(arg_keys[4], 1), 0, 1),
        "size_class": set_ends((jax.random.randint(arg_keys[5], (IMAGES,), 0, 11) < 3).astype(jnp.int32), jax.random.fold_in(arg_keys[5], 1), 0, 1),
        "proj_in": bell_draw(arg_keys[6], (C, C), C ** -0.5, 0.25, ((0, 32),)),
        "kernel_large": bell_draw(arg_keys[7], (KL, KL, C), (KL * KL) ** -0.5, 0.21875, ((2, 32),)),
        "kernel_small": bell_draw(arg_keys[8], (KS, KS, C), (KS * KS) ** -0.5, 1.25, ((2, 32),)),
        "proj_out": bell_draw(arg_keys[9], (C, C), C ** -0.5, 0.25, ((0, 32),)),
        "norm_gain": jnp.clip(1.0 + 0.18 * jax.random.normal(arg_keys[10], (5, C), jnp.float32), 0.099609375, 1.8984375).astype(jnp.bfloat16),
        "norm_bias": bell_draw(arg_keys[11], (5, C), 0.5, 2.0, ((1, 32),)),
        "ffn_up": bell_draw(arg_keys[12], (C, FF), C ** -0.5, 0.25, ((0, 16), (1, 2))),
        "ffn_down": bell_draw(arg_keys[13], (FF, C), FF ** -0.5, 0.125, ((0, 2), (1, 16))),
        "cotangent": bell_draw(arg_keys[14], (IMAGES, CANVAS, CANVAS, C), 1.0, 6.0, ((0, 32),)),
    }


EPS = 1e-05
HIGH = lax.Precision.HIGHEST

@jax.custom_vjp
def low(v):
    return lax.optimization_barrier(v.astype(jnp.bfloat16)).astype(jnp.float32)

@jax.custom_vjp
def low_back(v):
    return v

def low_keep(v):
    return (low(v), None)

def low_pass(kept, grad):
    return (grad,)

def back_keep(v):
    return (v, None)

def back_low(kept, grad):
    return (low(grad),)
low.defvjp(low_keep, low_pass)
low_back.defvjp(back_keep, back_low)

def region(image_sides):
    inside_line = jnp.arange(CANVAS)[None, :] < image_sides[:, None]
    return (inside_line[:, :, None] & inside_line[:, None, :]).astype(jnp.float32)[:, :, :, None]

def place_image(image_map, offset_pair, flip_bit, side_length):
    turned = jnp.where(flip_bit > 0, image_map[:, ::-1, :], image_map)
    padded = jnp.pad(turned, ((0, CANVAS), (0, CANVAS), (0, 0)))
    corner = jnp.minimum(offset_pair, CANVAS - side_length).astype(jnp.int32)
    anchor = jnp.zeros((), jnp.int32)
    return lax.dynamic_slice(padded, (corner[0], corner[1], anchor), (CANVAS, CANVAS, image_map.shape[2]))

def normalize(values, region_mask, pixels, gain_row, bias_row):
    totals = lax.optimization_barrier(jnp.sum(values * region_mask, axis=(0, 1, 2)))
    squares = lax.optimization_barrier(jnp.sum(values * values * region_mask, axis=(0, 1, 2)))
    average = totals / pixels
    inverse = lax.rsqrt(squares / pixels - average * average + EPS)
    return (values - average) * inverse * gain_row + bias_row

@jax.checkpoint
def activated(values, region_mask, pixels, gain_row, bias_row):
    return region_mask * jax.nn.gelu(normalize(values, region_mask, pixels, gain_row, bias_row))

@jax.checkpoint
def masked_norm(values, region_mask, pixels, gain_row, bias_row):
    return region_mask * normalize(values, region_mask, pixels, gain_row, bias_row)

def tap_table(extent):
    radius = (extent - 1) // 2
    row_of = np.arange(CANVAS * CANVAS) // CANVAS
    column_of = np.arange(CANVAS * CANVAS) % CANVAS
    vertical = row_of[:, None] - row_of[None, :]
    horizontal = column_of[:, None] - column_of[None, :]
    inside = (np.abs(vertical) <= radius) & (np.abs(horizontal) <= radius)
    position = np.where(inside, (vertical + radius) * extent + horizontal + radius, 0)
    return (position.astype(np.int32), inside.astype(np.float32))

def depthwise(spread, kernel):
    extent = kernel.shape[0]
    position, inside = tap_table(extent)
    group_size = 64
    image_count = spread.shape[0]
    columns = spread.reshape(image_count, CANVAS * CANVAS, C).transpose(2, 0, 1)
    columns = columns.reshape(C // group_size, group_size, image_count, CANVAS * CANVAS)
    kernel_rows = kernel.reshape(extent * extent, C).T.reshape(C // group_size, group_size, extent * extent)

    def per_group(operands):
        values, taps_here = operands
        matrix = taps_here[:, position] * inside
        return jnp.einsum('gnq,gqp->gnp', values, matrix, precision=HIGH)
    result = lax.map(jax.checkpoint(per_group), (columns, kernel_rows))
    result = result.reshape(C, image_count, CANVAS * CANVAS).transpose(1, 2, 0)
    return result.reshape(image_count, CANVAS, CANVAS, C)

def ffn_group(normed_part, ffn_up, ffn_down):
    hidden_pre = low_back(jnp.einsum('nhwc,cf->nhwf', normed_part, ffn_up, precision=HIGH))
    hidden = low(jax.nn.gelu(hidden_pre))
    return low_back(jnp.einsum('nhwf,fc->nhwc', hidden, ffn_down, precision=HIGH))

def feed_forward(normed, ffn_up, ffn_down):
    groups = normed.reshape(-1, 8, CANVAS, CANVAS, C)
    result = lax.map(lambda part_maps: jax.checkpoint(ffn_group)(part_maps, ffn_up, ffn_down), groups)
    return result.reshape(normed.shape)

def forward(raw_wide, proj_in, kernel_large, kernel_small, proj_out, gain_all, bias_all, ffn_up, ffn_down, partner, ratios, offsets, flip_bits, size_class):
    image_sides = SMALL + (CANVAS - SMALL) * size_class
    region_mask = region(image_sides)
    pixels = jnp.sum(region_mask)
    mix_weight = ratios[:, None, None, None]
    mixed_maps = mix_weight * raw_wide + (1.0 - mix_weight) * raw_wide[partner]
    inputs = region_mask * jax.vmap(place_image)(mixed_maps, offsets, flip_bits, image_sides)
    first_low = low(masked_norm(inputs, region_mask, pixels, gain_all[0], bias_all[0]))
    inner_pre = low_back(jnp.einsum('nhwc,cd->nhwd', first_low, proj_in, precision=HIGH))
    spread = low(activated(inner_pre, region_mask, pixels, gain_all[1], bias_all[1]))
    large_out = low_back(depthwise(spread, kernel_large))
    small_out = low_back(depthwise(spread, kernel_small))
    joined = normalize(large_out, region_mask, pixels, gain_all[2], bias_all[2])
    joined = joined + normalize(small_out, region_mask, pixels, gain_all[3], bias_all[3])
    merged = low(region_mask * jax.nn.gelu(joined))
    block_sum = inputs + low_back(jnp.einsum('nhwc,cd->nhwd', merged, proj_out, precision=HIGH))
    normed = low(masked_norm(block_sum, region_mask, pixels, gain_all[4], bias_all[4]))
    return block_sum + feed_forward(normed, ffn_up, ffn_down)

def reference(raw_maps, partner, ratios, offsets, flip_bits, size_class, proj_in, kernel_large, kernel_small, proj_out, norm_gain, norm_bias, ffn_up, ffn_down, cotangent):

    def wrapped(raw_wide, w_in, k_large, k_small, w_out, gain_all, bias_all, w_up, w_down):
        return forward(raw_wide, w_in, k_large, k_small, w_out, gain_all, bias_all, w_up, w_down, partner, ratios, offsets, flip_bits, size_class)
    primals = (raw_maps.astype(jnp.float32), proj_in.astype(jnp.float32), kernel_large.astype(jnp.float32), kernel_small.astype(jnp.float32), proj_out.astype(jnp.float32), norm_gain.astype(jnp.float32), norm_bias.astype(jnp.float32), ffn_up.astype(jnp.float32), ffn_down.astype(jnp.float32))
    output, pull_back = jax.vjp(wrapped, *primals)
    gradients = pull_back(cotangent.astype(jnp.float32))
    return (output.astype(jnp.bfloat16), gradients[0], gradients[1], gradients[2], gradients[3], gradients[4], gradients[5], gradients[6], gradients[7], gradients[8])
```

```python
import functools

import jax
import jax.numpy as jnp
import ml_dtypes
import numpy as np
from jax import lax
from jax.experimental import pallas as pl
from jax.experimental.pallas import tpu as pltpu
from jax.sharding import PartitionSpec as P

CANVAS = 24
SMALL = 14
SPOTS = CANVAS * CANVAS
EPS = 1e-05
BOTH = ("batch", "hid")
ROOT = float(np.sqrt(2.0 / np.pi))
CUBE = 0.044715
F32 = jnp.float32
BF16 = jnp.bfloat16
STEPS = 4
VMEM = 56 * 1024 * 1024


def frequencies(extent):
    side = CANVAS + (extent - 1) // 2
    half = [(0, v) for v in range(side // 2 + 1)]
    half += [(u, v) for u in range(1, side // 2 + 1) for v in range(side)]
    if side % 2 == 0:
        raise ValueError("even side")
    return side, np.array(half, np.float64)


def waves(points, extent, columns, scaled):
    side, half = frequencies(extent)
    count = -(-len(half) // 16) * 16
    angle = 2.0 * np.pi / side * (half @ np.array(points, np.float64).T)
    weight = np.where(np.arange(len(half)) == 0, 1.0, 2.0)[:, None] / side**2 if scaled else 1.0
    table = np.zeros((2 * count, columns), np.float64)
    table[: len(half), : len(points)] = np.cos(angle) * weight
    table[count : count + len(half), : len(points)] = np.sin(angle) * weight
    return table.astype(ml_dtypes.bfloat16)


def taps(extent):
    radius = (extent - 1) // 2
    return [(a - radius, b - radius) for a in range(extent) for b in range(extent)]


def padded(count):
    return -(-count // 128) * 128


def dot(a, b):
    return lax.dot_general(a, b, (((1,), (0,)), ((), ())), preferred_element_type=F32)


def dot_t(a, b):
    return lax.dot_general(a, b, (((1,), (1,)), ((), ())), preferred_element_type=F32)


def t_dot(a, b):
    return lax.dot_general(a, b, (((0,), (0,)), ((), ())), preferred_element_type=F32)


def gelu_parts(v):
    square = v * v
    bend = jnp.tanh(ROOT * v * (1.0 + CUBE * square))
    half = 0.5 + 0.5 * bend
    slope = half + (0.5 * ROOT) * v * (1.0 - bend * bend) * (1.0 + (3.0 * CUBE) * square)
    return v * half, slope


def gelu(v):
    return v * (0.5 + 0.5 * jnp.tanh(ROOT * v * (1.0 + CUBE * v * v)))


def center(totals, squares, pixels):
    average = totals / pixels
    return average, lax.rsqrt(squares / pixels - average * average + EPS)


def rows_of(*rows):
    return jnp.concatenate(rows, axis=0)


def down(v):
    return jnp.sum(v, axis=0, keepdims=True)


def tell(ref, rows):
    ref[...] = jnp.broadcast_to(rows[None], ref.shape)


def add_up(acc, step, rows):
    @pl.when(step == 0)
    def _():
        acc[...] = rows

    @pl.when(step > 0)
    def _():
        acc[...] += rows


def mix_kernel(images, rel, ratio, sides, own, first, second, target, x_out, st_out, other, acc):
    i = pl.program_id(0)

    @pl.when(rel[i] < images)
    def _():
        other[...] = first[0]

    @pl.when(rel[i] >= images)
    def _():
        other[...] = second[0]

    pick = (target[0] == lax.broadcasted_iota(jnp.int32, (SPOTS, SPOTS), 1)).astype(BF16)
    x = ratio[i] * dot(pick, own[0]) + (1.0 - ratio[i]) * dot(pick, other[...])
    x_out[0] = x
    pixels = jnp.full((1, x.shape[1]), (sides[i] * sides[i]).astype(F32), F32)
    add_up(acc, i, rows_of(down(x), down(x * x), pixels))

    @pl.when(i == images - 1)
    def _():
        tell(st_out, acc[...])


def inner_kernel(steps, st, gb, mask, x, w_in, first_out, inner_out, norm_out, st_out, coef, acc):
    i = pl.program_id(0)

    @pl.when(i == 0)
    def _():
        sums = jnp.sum(st[...], axis=0)
        pixels = sums[2:3]
        average, inverse = center(sums[0:1], sums[1:2], pixels)
        coef[...] = rows_of(average, inverse, pixels)
        norm_out[...] = coef[...]

    scale = coef[1:2] * gb[0:1]
    shift = gb[5:6] - coef[0:1] * scale
    first = ((x[...] * scale + shift) * mask[...]).astype(BF16)
    first_out[...] = first
    inner = dot(first, w_in[...])
    inner_out[...] = inner
    inner = inner * mask[...]
    add_up(acc, i, rows_of(down(inner), down(inner * inner)))

    @pl.when(i == steps - 1)
    def _():
        tell(st_out, acc[...])


def taps_kernel(kt, waves_large, waves_small, large_out, small_out):
    large = waves_large.shape[1]
    large_out[...] = dot_t(waves_large[...], kt[:, :large])
    small_out[...] = dot_t(waves_small[...], kt[:, large:])


def spread_kernel(
    images, st, norm, gb, mask, inner, fourier, back, tap_large, tap_small,
    large_out, small_out, moved_out, norm_out, st_out,
):
    sums = jnp.sum(st[...], axis=0)
    pixels = norm[2:3]
    average, inverse = center(sums[0:1], sums[1:2], pixels)
    norm_out[...] = rows_of(average, inverse)
    scale = inverse * gb[1:2]
    shift = gb[6:7] - average * scale
    half = fourier.shape[0] // 2
    totals = None
    for n in range(images):
        rows = slice(n * SPOTS, (n + 1) * SPOTS)
        here = mask[rows]
        spread = (gelu(inner[rows] * scale + shift) * here).astype(BF16)
        moved = dot(fourier[...], spread)
        moved_out[n] = moved
        mc, ms = moved[:half], moved[half:]
        outs = []
        for tap in (tap_large, tap_small):
            kc, ks = tap[:half], tap[half:]
            both = jnp.concatenate(
                [(mc * kc + ms * ks).astype(BF16), (ms * kc - mc * ks).astype(BF16)], axis=0
            )
            outs.append(dot(back[...], both))
        large_out[rows] = outs[0]
        small_out[rows] = outs[1]
        large, small = outs[0] * here, outs[1] * here
        part = rows_of(down(large), down(large * large), down(small), down(small * small))
        totals = part if totals is None else totals + part
    tell(st_out, totals)


def merge_kernel(steps, st, norm, gb, mask, large, small, x, w_out, merged_out, block_out, norm_out, st_out, coef, acc):
    i = pl.program_id(0)

    @pl.when(i == 0)
    def _():
        sums = jnp.sum(st[...], axis=0)
        pixels = norm[2:3]
        coef[...] = rows_of(*center(sums[0:1], sums[1:2], pixels), *center(sums[2:3], sums[3:4], pixels))
        norm_out[...] = coef[...]

    by_large = coef[1:2] * gb[2:3]
    by_small = coef[3:4] * gb[3:4]
    shift = gb[7:8] + gb[8:9] - coef[0:1] * by_large - coef[2:3] * by_small
    pre = large[...] * by_large + small[...] * by_small + shift
    merged = (gelu(pre) * mask[...]).astype(BF16)
    merged_out[...] = merged
    block = x[...] + dot(merged, w_out[...])
    block_out[...] = block
    block = block * mask[...]
    add_up(acc, i, rows_of(down(block), down(block * block)))

    @pl.when(i == steps - 1)
    def _():
        tell(st_out, acc[...])


def ffn_kernel(
    steps, st, norm, gb, mask, block, ct, up, dn,
    out, gn_out, norm_out, st_out, gup_out, gdn_out,
    normed, normed_t, ct_t, branch, gn, coef,
):
    j = pl.program_id(0)

    @pl.when(j == 0)
    def _():
        sums = jnp.sum(st[...], axis=0)
        coef[...] = rows_of(*center(sums[0:1], sums[1:2], norm[2:3]))
        norm_out[...] = coef[...]
        scale = coef[1:2] * gb[4:5]
        shift = gb[9:10] - coef[0:1] * scale
        value = ((block[...] * scale + shift) * mask[...]).astype(BF16)
        normed[...] = value
        normed_t[...] = value.T
        ct_t[...] = ct[...].T
        branch[...] = jnp.zeros_like(branch)
        gn[...] = jnp.zeros_like(gn)

    hidden, slope = gelu_parts(dot(normed[...], up[0]))
    hidden = hidden.astype(BF16)
    branch[...] += dot_t(hidden, dn[0])
    gdn_out[0] = dot(ct_t[...], hidden).astype(BF16)
    grad = (slope * dot(ct[...], dn[0])).astype(BF16)
    gup_out[0] = dot(normed_t[...], grad).astype(BF16)
    gn[...] += dot_t(grad, up[0])

    @pl.when(j == steps - 1)
    def _():
        out[...] = (block[...] + branch[...]).astype(BF16)
        masked = gn[...] * mask[...]
        gn_out[...] = masked
        normal = (block[...] - coef[0:1]) * coef[1:2]
        tell(st_out, rows_of(down(masked), down(masked * normal)))


def merge_back_kernel(
    steps, st, norm, norm_two, norm_four, gb, mask, block, gn, ct, merged, large, small, w_out,
    gblock_out, gout_out, g_out, sums_out, st_out, coef, acc, gw,
):
    i = pl.program_id(0)

    @pl.when(i == 0)
    def _():
        coef[...] = jnp.sum(st[...], axis=0)
        sums_out[...] = coef[...]

    average, inverse = norm_four[0:1], norm_four[1:2]
    normal = (block[...] - average) * inverse
    here = mask[...]
    inside = gn[...] - (coef[0:1] + normal * coef[1:2]) / norm[2:3]
    gblock = ct[...].astype(F32) + here * (gb[4:5] * inverse * inside)
    gblock_out[...] = gblock
    branch = gblock.astype(BF16)
    add_up(gw, i, t_dot(merged[...], branch))
    v_large = (large[...] - norm_two[0:1]) * norm_two[1:2]
    v_small = (small[...] - norm_two[2:3]) * norm_two[3:4]
    pre = v_large * gb[2:3] + v_small * gb[3:4] + (gb[7:8] + gb[8:9])
    _, slope = gelu_parts(pre)
    g = here * slope * dot_t(branch, w_out[...])
    g_out[...] = g
    add_up(acc, i, rows_of(down(g), down(g * v_large), down(g * v_small)))

    @pl.when(i == steps - 1)
    def _():
        tell(st_out, acc[...])
        gout_out[...] = gw[...].astype(BF16)


def spread_back_kernel(
    images, st, norm, norm_one, norm_two, gb, mask, inner, large, small, g, moved, fourier, back,
    tap_large, tap_small, waves_large, waves_small, g_out, gk_out, sums_out, st_out,
):
    sums = jnp.sum(st[...], axis=0)
    sums_out[...] = sums
    pixels = norm[2:3]
    by_bias = sums[0:1] / pixels
    half = fourier.shape[0] // 2
    totals = None
    kernel_moved = [None, None]
    for n in range(images):
        rows = slice(n * SPOTS, (n + 1) * SPOTS)
        here = mask[rows]
        sc, ss = moved[n, :half], moved[n, half:]
        total_c = total_s = None
        for k, (value, tap) in enumerate(((large, tap_large), (small, tap_small))):
            average, inverse = norm_two[2 * k : 2 * k + 1], norm_two[2 * k + 1 : 2 * k + 2]
            normal = (value[rows] - average) * inverse
            inside = g[rows] - (by_bias + normal * (sums[1 + k : 2 + k] / pixels))
            gradient = (here * (gb[2 + k : 3 + k] * inverse * inside)).astype(BF16)
            change = dot(fourier[...], gradient)
            gc, gs = change[:half], change[half:]
            kc, ks = tap[:half], tap[half:]
            real, imag = gc * kc - gs * ks, gc * ks + gs * kc
            total_c = real if k == 0 else total_c + real
            total_s = imag if k == 0 else total_s + imag
            real, imag = sc * gc + ss * gs, ss * gc - sc * gs
            pair = kernel_moved[k]
            kernel_moved[k] = (real, imag) if n == 0 else (pair[0] + real, pair[1] + imag)
        both = jnp.concatenate([total_c.astype(BF16), total_s.astype(BF16)], axis=0)
        grad_spread = dot(back[...], both)
        normal = (inner[rows] - norm_one[0:1]) * norm_one[1:2]
        _, slope = gelu_parts(normal * gb[1:2] + gb[6:7])
        first = here * slope * grad_spread
        g_out[rows] = first
        part = rows_of(down(first), down(first * normal))
        totals = part if n == 0 else totals + part
    tell(st_out, totals)
    for k, table in enumerate((waves_large, waves_small)):
        real, imag = kernel_moved[k]
        both = jnp.concatenate([real.astype(BF16), imag.astype(BF16)], axis=0)
        width = waves_large.shape[1]
        place = slice(0, width) if k == 0 else slice(width, width + table.shape[1])
        gk_out[:, place] = t_dot(both, table[...]).astype(BF16)


def inner_back_kernel(
    steps, st, norm, norm_one, gb, mask, inner, g, first, x, w_in,
    gf_out, gin_out, sums_out, st_out, coef, acc, gw,
):
    i = pl.program_id(0)

    @pl.when(i == 0)
    def _():
        coef[...] = jnp.sum(st[...], axis=0)
        sums_out[...] = coef[...]

    average, inverse = norm_one[0:1], norm_one[1:2]
    normal = (inner[...] - average) * inverse
    here = mask[...]
    inside = g[...] - (coef[0:1] + normal * coef[1:2]) / norm[2:3]
    grad = (here * (gb[1:2] * inverse * inside)).astype(BF16)
    add_up(gw, i, t_dot(first[...], grad))
    gf = here * dot_t(grad, w_in[...])
    gf_out[...] = gf
    add_up(acc, i, rows_of(down(gf), down(gf * ((x[...] - norm[0:1]) * norm[1:2]))))

    @pl.when(i == steps - 1)
    def _():
        tell(st_out, acc[...])
        gin_out[...] = gw[...].astype(BF16)


def unmix_kernel(images, rel, ratio, st, norm, gb, mask, gblock, gf, x, target, own_out, prev_out, sums_out, prev, coef):
    i = pl.program_id(0)

    @pl.when(i == 0)
    def _():
        coef[...] = jnp.sum(st[...], axis=0)
        sums_out[...] = coef[...]
        prev[...] = jnp.zeros_like(prev)
        own_out[...] = jnp.zeros_like(own_out)

    normal = (x[0] - norm[0:1]) * norm[1:2]
    inside = gf[0] - (coef[0:1] + normal * coef[1:2]) / norm[2:3]
    grad = (mask[...] * (gblock[0] + gb[0:1] * norm[1:2] * inside)).astype(BF16)
    pick = (target[0] == lax.broadcasted_iota(jnp.int32, (SPOTS, SPOTS), 0)).astype(BF16)
    grad = dot(pick, grad)
    own_out[i] += ratio[i] * grad
    giving = (1.0 - ratio[i]) * grad
    to = rel[i]

    @pl.when(to < images)
    def _():
        prev[jnp.minimum(to, images - 1)] += giving

    @pl.when(to >= images)
    def _():
        own_out[jnp.maximum(to - images, 0)] += giving

    @pl.when(i == images - 1)
    def _():
        prev_out[...] = prev[...].astype(BF16)


def shape(dims, kind=F32):
    return jax.ShapeDtypeStruct(dims, kind)


def whole(dims):
    return pl.BlockSpec(dims, lambda *_: (0,) * len(dims))


def by_rows(rows, columns):
    return pl.BlockSpec((rows, columns), lambda i: (i, 0))


def params():
    return pltpu.CompilerParams(vmem_limit_bytes=VMEM)


def shifted(block, distance):
    count = lax.axis_size(BOTH)
    return lax.ppermute(block, BOTH, [((i - distance) % count, i) for i in range(count)])


def exchange(parts):
    return lax.all_to_all(parts, BOTH, 0, 0)


def shards(
    raw_maps, partner, ratios, offsets, flip_bits, size_class, proj_in, kernel_large, kernel_small,
    proj_out, norm_gain, norm_bias, ffn_up, ffn_down, cotangent,
):
    images, channels = raw_maps.shape[0], raw_maps.shape[3]
    share = proj_in.shape[0]
    count = lax.axis_size(BOTH)
    position = lax.axis_index(BOTH)
    pixels_here = images * SPOTS
    rows = pixels_here // STEPS
    large_extent, small_extent = kernel_large.shape[0], kernel_small.shape[0]
    large_taps, small_taps = large_extent**2, small_extent**2
    large_wide, small_wide = padded(large_taps), padded(small_taps)
    spots = [(r, c) for r in range(CANVAS) for c in range(CANVAS)]
    fourier_np = waves(spots, large_extent, SPOTS, False)
    fourier, back = jnp.asarray(fourier_np), jnp.asarray(np.ascontiguousarray(fourier_np.T))
    waves_large = jnp.asarray(waves(taps(large_extent), large_extent, large_wide, True))
    waves_small = jnp.asarray(waves(taps(small_extent), large_extent, small_wide, True))
    bins = fourier_np.shape[0]

    raw = raw_maps.reshape(images, SPOTS, channels)
    ct = cotangent.reshape(pixels_here, channels)
    earlier = shifted(raw, 1)

    norms = jnp.pad(jnp.concatenate([norm_gain, norm_bias], axis=0).T, ((0, 0), (0, 118)))
    early = exchange(jnp.broadcast_to(jnp.concatenate([proj_in, norms], axis=1)[None], (count, share, channels + 128)))
    early = early.reshape(channels, channels + 128)
    w_in = early[:, :channels]
    gb = early[:, channels : channels + 16].T.astype(F32)
    taps_here = jnp.concatenate(
        [
            jnp.pad(kernel_large.reshape(large_taps, share).T, ((0, 0), (0, large_wide - large_taps))),
            jnp.pad(kernel_small.reshape(small_taps, share).T, ((0, 0), (0, small_wide - small_taps))),
            proj_out,
        ],
        axis=1,
    )
    middle = lax.all_gather(taps_here, BOTH, axis=0, tiled=True)
    kt, w_out = middle[:, : large_wide + small_wide], middle[:, large_wide + small_wide :]
    hidden_here = ffn_up.shape[1]
    ffn_own = lax.all_gather(jnp.concatenate([ffn_up, ffn_down.T], axis=1), "batch", axis=0, tiled=True)
    swap = [(0, 1), (1, 0)]
    ffn = jnp.stack([ffn_own, lax.ppermute(ffn_own, "hid", swap)])

    sides = SMALL + (CANVAS - SMALL) * size_class
    spot = lax.broadcasted_iota(jnp.int32, (images, SPOTS), 1)
    row, column = spot // CANVAS, spot % CANVAS
    inside = (row < sides[:, None]) & (column < sides[:, None])
    corner = jnp.minimum(offsets, (CANVAS - sides)[:, None])
    source = column + corner[:, 1:2]
    source = jnp.where(flip_bits[:, None] > 0, CANVAS - 1 - source, source)
    target = jnp.where(inside, (row + corner[:, 0:1]) * CANVAS + source, -1)
    mask = inside.astype(F32).reshape(pixels_here, 1)
    relative = jnp.mod(partner - (position * images - images), count * images)

    def stats(k):
        return shape((count, k, channels)), whole((count, k, channels))

    def call(kernel, grid, ins, in_specs, outs, out_specs, scratch=(), prefetch=0):
        spec = pltpu.PrefetchScalarGridSpec(
            num_scalar_prefetch=prefetch, grid=grid, in_specs=in_specs, out_specs=out_specs, scratch_shapes=list(scratch)
        )
        return pl.pallas_call(kernel, grid_spec=spec, out_shape=outs, compiler_params=params())(*ins)

    row_c = by_rows(rows, channels)
    row_1 = by_rows(rows, 1)
    map_f = shape((pixels_here, channels))
    map_b = shape((pixels_here, channels), BF16)
    norm_spec = whole((3, channels))
    gb_spec = whole((16, channels))
    square = whole((channels, channels))
    image_spec = pl.BlockSpec((1, SPOTS, channels), lambda i, *_: (i, 0, 0))
    image_f = shape((images, SPOTS, channels))

    shape3, spec3 = stats(3)
    x, st = call(
        functools.partial(mix_kernel, images),
        (images,),
        (relative, ratios, sides, raw, earlier, raw, target[:, :, None]),
        [
            image_spec,
            pl.BlockSpec((1, SPOTS, channels), lambda i, rel, *_: (jnp.minimum(rel[i], images - 1), 0, 0)),
            pl.BlockSpec((1, SPOTS, channels), lambda i, rel, *_: (jnp.maximum(rel[i] - images, 0), 0, 0)),
            pl.BlockSpec((1, SPOTS, 1), lambda i, *_: (i, 0, 0)),
        ],
        (image_f, shape3),
        (image_spec, spec3),
        [pltpu.VMEM((SPOTS, channels), BF16), pltpu.VMEM((3, channels), F32)],
        prefetch=3,
    )
    x = x.reshape(pixels_here, channels)
    st = exchange(st)

    shape2, spec2 = stats(2)
    first, inner, norm, st = call(
        functools.partial(inner_kernel, STEPS),
        (STEPS,),
        (st, gb, mask, x, w_in),
        [spec3, gb_spec, row_1, row_c, square],
        (map_b, map_f, shape((3, channels)), shape2),
        (row_c, row_c, norm_spec, spec2),
        [pltpu.VMEM((3, channels), F32), pltpu.VMEM((2, channels), F32)],
    )
    st = exchange(st)

    chunk = 256 if channels % 256 == 0 else channels
    chunks = channels // chunk
    tap_shape = shape((bins, channels))
    tap_spec = pl.BlockSpec((bins, chunk), lambda i: (0, i))
    kt_spec = pl.BlockSpec((chunk, large_wide + small_wide), lambda i: (i, 0))
    wl_spec, ws_spec = whole((bins, large_wide)), whole((bins, small_wide))
    tap_large, tap_small = call(
        taps_kernel,
        (chunks,),
        (kt, waves_large, waves_small),
        [kt_spec, wl_spec, ws_spec],
        (tap_shape, tap_shape),
        (tap_spec, tap_spec),
    )

    def chunk_stats(k):
        return pl.BlockSpec((count, k, chunk), lambda i: (0, 0, i))

    def chunk_rows(k):
        return pl.BlockSpec((k, chunk), lambda i: (0, i))

    four_spec, back_spec = whole((bins, SPOTS)), whole((SPOTS, bins))
    mask_spec = whole((pixels_here, 1))
    shape4, spec4 = stats(4)
    moved_spec = pl.BlockSpec((images, bins, chunk), lambda i: (0, 0, i))
    large, small, moved, norm_one, st = call(
        functools.partial(spread_kernel, images),
        (chunks,),
        (st, norm, gb, mask, inner, fourier, back, tap_large, tap_small),
        [chunk_stats(2), chunk_rows(3), chunk_rows(16), mask_spec, chunk_rows(pixels_here), four_spec, back_spec, tap_spec, tap_spec],
        (map_f, map_f, shape((images, bins, channels)), shape((2, channels)), shape4),
        (chunk_rows(pixels_here), chunk_rows(pixels_here), moved_spec, chunk_rows(2), chunk_stats(4)),
    )
    st = exchange(st)

    merged, block, norm_two, st = call(
        functools.partial(merge_kernel, STEPS),
        (STEPS,),
        (st, norm, gb, mask, large, small, x, w_out),
        [spec4, norm_spec, gb_spec, row_1, row_c, row_c, row_c, square],
        (map_b, map_f, shape((4, channels)), shape2),
        (row_c, row_c, whole((4, channels)), spec2),
        [pltpu.VMEM((4, channels), F32), pltpu.VMEM((2, channels), F32)],
    )
    st = exchange(st)

    wide = 256 if hidden_here % 256 == 0 else hidden_here
    per_half = hidden_here // wide
    steps = 2 * per_half
    map_spec = whole((pixels_here, channels))
    up_spec = pl.BlockSpec((1, channels, wide), lambda j: (j // per_half, 0, j % per_half))
    dn_spec = pl.BlockSpec((1, channels, wide), lambda j: (j // per_half, 0, per_half + j % per_half))
    gw_shape = shape((2, channels, hidden_here), BF16)
    output, gn, norm_four, st, gup, gdn = call(
        functools.partial(ffn_kernel, steps),
        (steps,),
        (st, norm, gb, mask, block, ct, ffn, ffn),
        [spec2, norm_spec, gb_spec, mask_spec, map_spec, map_spec, up_spec, dn_spec],
        (map_b, map_f, shape((2, channels)), shape2, gw_shape, gw_shape),
        (map_spec, map_spec, whole((2, channels)), spec2, up_spec, up_spec),
        [
            pltpu.VMEM((pixels_here, channels), BF16),
            pltpu.VMEM((channels, pixels_here), BF16),
            pltpu.VMEM((channels, pixels_here), BF16),
            pltpu.VMEM((pixels_here, channels), F32),
            pltpu.VMEM((pixels_here, channels), F32),
            pltpu.VMEM((2, channels), F32),
        ],
    )
    st = exchange(st)
    gffn_other = jnp.concatenate([gup[1], gdn[1]], axis=1)
    gffn = jnp.concatenate([gup[0], gdn[0]], axis=1).astype(F32)
    gffn = (gffn + lax.ppermute(gffn_other, "hid", swap).astype(F32)).astype(BF16)
    gffn = lax.psum_scatter(gffn, "batch", scatter_dimension=0, tiled=True).astype(F32)

    gw_here = shape((channels, channels), BF16)
    gblock, gout, g, sums_four, st = call(
        functools.partial(merge_back_kernel, STEPS),
        (STEPS,),
        (st, norm, norm_two, norm_four, gb, mask, block, gn, ct, merged, large, small, w_out),
        [spec2, norm_spec, whole((4, channels)), whole((2, channels)), gb_spec, row_1] + [row_c] * 6 + [square],
        (map_f, gw_here, map_f, shape((2, channels)), shape3),
        (row_c, square, row_c, whole((2, channels)), spec3),
        [pltpu.VMEM((2, channels), F32), pltpu.VMEM((3, channels), F32), pltpu.VMEM((channels, channels), F32)],
    )
    st = exchange(st)

    gk_shape = shape((channels, large_wide + small_wide), BF16)
    map_chunk = chunk_rows(pixels_here)
    g, gk, sums_two, st = call(
        functools.partial(spread_back_kernel, images),
        (chunks,),
        (st, norm, norm_one, norm_two, gb, mask, inner, large, small, g, moved, fourier, back, tap_large, tap_small, waves_large, waves_small),
        [chunk_stats(3), chunk_rows(3), chunk_rows(2), chunk_rows(4), chunk_rows(16), mask_spec, map_chunk, map_chunk, map_chunk, map_chunk,
         moved_spec, four_spec, back_spec, tap_spec, tap_spec, wl_spec, ws_spec],
        (map_f, gk_shape, shape((3, channels)), shape2),
        (map_chunk, kt_spec, chunk_rows(3), chunk_stats(2)),
    )
    st = exchange(st)
    gmiddle = jnp.concatenate([gk, gout], axis=1).reshape(count, share, large_wide + small_wide + channels)
    gmiddle = jnp.sum(exchange(gmiddle).astype(F32), axis=0)

    gf, gin, sums_one, st = call(
        functools.partial(inner_back_kernel, STEPS),
        (STEPS,),
        (st, norm, norm_one, gb, mask, inner, g, first, x, w_in),
        [spec2, norm_spec, whole((2, channels)), gb_spec, row_1, row_c, row_c, row_c, row_c, square],
        (map_f, gw_here, shape((2, channels)), shape2),
        (row_c, square, whole((2, channels)), spec2),
        [pltpu.VMEM((2, channels), F32), pltpu.VMEM((2, channels), F32), pltpu.VMEM((channels, channels), F32)],
    )
    st = exchange(st)
    gin = jnp.sum(exchange(gin.reshape(count, share, channels)).astype(F32), axis=0)

    all_images = whole((images, SPOTS, channels))
    own, prev, sums_zero = call(
        functools.partial(unmix_kernel, images),
        (images,),
        (
            relative, ratios, st, norm, gb, mask, gblock.reshape(images, SPOTS, channels),
            gf.reshape(images, SPOTS, channels), x.reshape(images, SPOTS, channels), target[:, None, :],
        ),
        [
            spec2, norm_spec, gb_spec, pl.BlockSpec((SPOTS, 1), lambda i, *_: (i, 0)), image_spec, image_spec, image_spec,
            pl.BlockSpec((1, 1, SPOTS), lambda i, *_: (i, 0, 0)),
        ],
        (image_f, shape((images, SPOTS, channels), BF16), shape((2, channels))),
        (all_images, all_images, whole((2, channels))),
        [pltpu.VMEM((images, SPOTS, channels), F32), pltpu.VMEM((2, channels), F32)],
        prefetch=2,
    )
    grad_raw = own + shifted(prev, -1).astype(F32)

    gains = jnp.concatenate([sums_zero[1:2], sums_one[1:2], sums_two[1:3], sums_four[1:2]], axis=0)
    biases = jnp.concatenate([sums_zero[0:1], sums_one[0:1], sums_two[0:1], sums_two[0:1], sums_four[0:1]], axis=0)
    canvas = (images, CANVAS, CANVAS, channels)
    return (
        output.reshape(canvas),
        grad_raw.reshape(canvas),
        gin,
        gmiddle[:, :large_taps].T.reshape(large_extent, large_extent, share),
        gmiddle[:, large_wide : large_wide + small_taps].T.reshape(small_extent, small_extent, share),
        gmiddle[:, large_wide + small_wide :],
        lax.dynamic_slice_in_dim(gains, position * share, share, 1),
        lax.dynamic_slice_in_dim(biases, position * share, share, 1),
        gffn[:, :hidden_here],
        gffn[:, hidden_here:].T,
    )


def solution(mesh):
    one = P(BOTH)
    maps = P(BOTH, None, None, None)
    flat = P(BOTH, None)
    kernels = P(None, None, BOTH)
    norms = P(None, BOTH)
    return jax.shard_map(
        shards,
        mesh=mesh,
        in_specs=(
            maps, one, one, flat, one, one, flat, kernels, kernels, flat, norms, norms,
            P("batch", "hid"), P("hid", "batch"), maps,
        ),
        out_specs=(maps, maps, flat, kernels, kernels, flat, norms, norms, P("batch", "hid"), P("hid", "batch")),
        check_vma=False,
    )
```

```python
import functools

import jax
import jax.numpy as jnp
import ml_dtypes
import numpy as np
from jax import lax
from jax.experimental import pallas as pl
from jax.experimental.pallas import tpu as pltpu
from jax.sharding import PartitionSpec as P

CANVAS = 24
SMALL = 14
SPOTS = CANVAS * CANVAS
EPS = 1e-05
BOTH = ("batch", "hid")
ROOT = float(np.sqrt(2.0 / np.pi))
CUBE = 0.044715
F32 = jnp.float32
BF16 = jnp.bfloat16
STEPS = 4
VMEM = 56 * 1024 * 1024


def frequencies(extent):
    side = CANVAS + (extent - 1) // 2
    half = [(0, v) for v in range(side // 2 + 1)]
    half += [(u, v) for u in range(1, side // 2 + 1) for v in range(side)]
    if side % 2 == 0:
        raise ValueError("even side")
    return side, np.array(half, np.float64)


def waves(points, extent, columns, scaled):
    side, half = frequencies(extent)
    count = -(-len(half) // 16) * 16
    angle = 2.0 * np.pi / side * (half @ np.array(points, np.float64).T)
    weight = np.where(np.arange(len(half)) == 0, 1.0, 2.0)[:, None] / side**2 if scaled else 1.0
    table = np.zeros((2 * count, columns), np.float64)
    table[: len(half), : len(points)] = np.cos(angle) * weight
    table[count : count + len(half), : len(points)] = np.sin(angle) * weight
    return table.astype(ml_dtypes.bfloat16)


def taps(extent):
    radius = (extent - 1) // 2
    return [(a - radius, b - radius) for a in range(extent) for b in range(extent)]


def padded(count):
    return -(-count // 128) * 128


def dot(a, b):
    return lax.dot_general(a, b, (((1,), (0,)), ((), ())), preferred_element_type=F32)


def dot_t(a, b):
    return lax.dot_general(a, b, (((1,), (1,)), ((), ())), preferred_element_type=F32)


def t_dot(a, b):
    return lax.dot_general(a, b, (((0,), (0,)), ((), ())), preferred_element_type=F32)


def gelu_parts(v):
    square = v * v
    bend = jnp.tanh(ROOT * v * (1.0 + CUBE * square))
    half = 0.5 + 0.5 * bend
    slope = half + (0.5 * ROOT) * v * (1.0 - bend * bend) * (1.0 + (3.0 * CUBE) * square)
    return v * half, slope


def gelu(v):
    return v * (0.5 + 0.5 * jnp.tanh(ROOT * v * (1.0 + CUBE * v * v)))


def center(totals, squares, pixels):
    average = totals / pixels
    return average, lax.rsqrt(squares / pixels - average * average + EPS)


def rows_of(*rows):
    return jnp.concatenate(rows, axis=0)


def down(v):
    return jnp.sum(v, axis=0, keepdims=True)


def tell(ref, rows):
    ref[...] = jnp.broadcast_to(rows[None], ref.shape)


def add_up(acc, step, rows):
    @pl.when(step == 0)
    def _():
        acc[...] = rows

    @pl.when(step > 0)
    def _():
        acc[...] += rows


def mix_kernel(images, rel, ratio, sides, own, first, second, target, x_out, st_out, other, acc):
    i = pl.program_id(0)

    @pl.when(rel[i] < images)
    def _():
        other[...] = first[0]

    @pl.when(rel[i] >= images)
    def _():
        other[...] = second[0]

    pick = (target[0] == lax.broadcasted_iota(jnp.int32, (SPOTS, SPOTS), 1)).astype(BF16)
    x = ratio[i] * dot(pick, own[0]) + (1.0 - ratio[i]) * dot(pick, other[...])
    x_out[0] = x
    pixels = jnp.full((1, x.shape[1]), (sides[i] * sides[i]).astype(F32), F32)
    add_up(acc, i, rows_of(down(x), down(x * x), pixels))

    @pl.when(i == images - 1)
    def _():
        tell(st_out, acc[...])


def inner_kernel(steps, st, gb, mask, x, w_in, first_out, inner_out, norm_out, st_out, coef, acc):
    i = pl.program_id(0)

    @pl.when(i == 0)
    def _():
        sums = jnp.sum(st[...], axis=0)
        pixels = sums[2:3]
        average, inverse = center(sums[0:1], sums[1:2], pixels)
        coef[...] = rows_of(average, inverse, pixels)
        norm_out[...] = coef[...]

    scale = coef[1:2] * gb[0:1]
    shift = gb[5:6] - coef[0:1] * scale
    first = ((x[...] * scale + shift) * mask[...]).astype(BF16)
    first_out[...] = first
    inner = dot(first, w_in[...])
    inner_out[...] = inner
    inner = inner * mask[...]
    add_up(acc, i, rows_of(down(inner), down(inner * inner)))

    @pl.when(i == steps - 1)
    def _():
        tell(st_out, acc[...])


def taps_kernel(kt, waves_large, waves_small, large_out, small_out):
    large = waves_large.shape[1]
    large_out[...] = dot_t(waves_large[...], kt[:, :large])
    small_out[...] = dot_t(waves_small[...], kt[:, large:])


def spread_kernel(
    images, st, norm, gb, mask, inner, fourier, back, tap_large, tap_small,
    large_out, small_out, moved_out, norm_out, st_out,
):
    sums = jnp.sum(st[...], axis=0)
    pixels = norm[2:3]
    average, inverse = center(sums[0:1], sums[1:2], pixels)
    norm_out[...] = rows_of(average, inverse)
    scale = inverse * gb[1:2]
    shift = gb[6:7] - average * scale
    half = fourier.shape[0] // 2
    totals = None
    for n in range(images):
        rows = slice(n * SPOTS, (n + 1) * SPOTS)
        here = mask[rows]
        spread = (gelu(inner[rows] * scale + shift) * here).astype(BF16)
        moved = dot(fourier[...], spread)
        moved_out[n] = moved
        mc, ms = moved[:half], moved[half:]
        outs = []
        for tap in (tap_large, tap_small):
            kc, ks = tap[:half], tap[half:]
            both = jnp.concatenate(
                [(mc * kc + ms * ks).astype(BF16), (ms * kc - mc * ks).astype(BF16)], axis=0
            )
            outs.append(dot(back[...], both))
        large_out[rows] = outs[0]
        small_out[rows] = outs[1]
        large, small = outs[0] * here, outs[1] * here
        part = rows_of(down(large), down(large * large), down(small), down(small * small))
        totals = part if totals is None else totals + part
    tell(st_out, totals)


def merge_kernel(steps, st, norm, gb, mask, large, small, x, w_out, merged_out, block_out, norm_out, st_out, coef, acc):
    i = pl.program_id(0)

    @pl.when(i == 0)
    def _():
        sums = jnp.sum(st[...], axis=0)
        pixels = norm[2:3]
        coef[...] = rows_of(*center(sums[0:1], sums[1:2], pixels), *center(sums[2:3], sums[3:4], pixels))
        norm_out[...] = coef[...]

    by_large = coef[1:2] * gb[2:3]
    by_small = coef[3:4] * gb[3:4]
    shift = gb[7:8] + gb[8:9] - coef[0:1] * by_large - coef[2:3] * by_small
    pre = large[...] * by_large + small[...] * by_small + shift
    merged = (gelu(pre) * mask[...]).astype(BF16)
    merged_out[...] = merged
    block = x[...] + dot(merged, w_out[...])
    block_out[...] = block
    block = block * mask[...]
    add_up(acc, i, rows_of(down(block), down(block * block)))

    @pl.when(i == steps - 1)
    def _():
        tell(st_out, acc[...])


def ffn_kernel(
    steps, wide, st, norm, gb, mask, block, ct, own_a, own_b, other_a, other_b,
    out, gn_out, norm_out, st_out, gown_out, gother_out,
    normed, normed_t, ct_t, branch, gn, coef, w, gw,
):
    j = pl.program_id(0)

    @pl.when(j == 0)
    def _():
        sums = jnp.sum(st[...], axis=0)
        coef[...] = rows_of(*center(sums[0:1], sums[1:2], norm[2:3]))
        norm_out[...] = coef[...]
        scale = coef[1:2] * gb[4:5]
        shift = gb[9:10] - coef[0:1] * scale
        value = ((block[...] * scale + shift) * mask[...]).astype(BF16)
        normed[...] = value
        normed_t[...] = value.T
        ct_t[...] = ct[...].T
        branch[...] = jnp.zeros_like(branch)
        gn[...] = jnp.zeros_like(gn)

    for quarter, part in enumerate((own_a, own_b, other_a, other_b)):

        @pl.when(j // (steps // 4) == quarter)
        def _():
            w[...] = part[...]

    up, dn = w[:, :wide], w[:, wide:]
    hidden, slope = gelu_parts(dot(normed[...], up))
    hidden = hidden.astype(BF16)
    branch[...] += dot_t(hidden, dn)
    gw[:, wide:] = dot(ct_t[...], hidden).astype(BF16)
    grad = (slope * dot(ct[...], dn)).astype(BF16)
    gw[:, :wide] = dot(normed_t[...], grad).astype(BF16)
    gn[...] += dot_t(grad, up)

    @pl.when(j < steps // 2)
    def _():
        gown_out[...] = gw[...]

    @pl.when(j >= steps // 2)
    def _():
        gother_out[...] = gw[...]

    @pl.when(j == steps - 1)
    def _():
        out[...] = (block[...] + branch[...]).astype(BF16)
        masked = gn[...] * mask[...]
        gn_out[...] = masked
        normal = (block[...] - coef[0:1]) * coef[1:2]
        tell(st_out, rows_of(down(masked), down(masked * normal)))


def merge_back_kernel(
    steps, st, norm, norm_two, norm_four, gb, mask, block, gn, ct, merged, large, small, w_out,
    gblock_out, gout_out, g_out, sums_out, st_out, coef, acc, gw,
):
    i = pl.program_id(0)

    @pl.when(i == 0)
    def _():
        coef[...] = jnp.sum(st[...], axis=0)
        sums_out[...] = coef[...]

    average, inverse = norm_four[0:1], norm_four[1:2]
    normal = (block[...] - average) * inverse
    here = mask[...]
    inside = gn[...] - (coef[0:1] + normal * coef[1:2]) / norm[2:3]
    gblock = ct[...].astype(F32) + here * (gb[4:5] * inverse * inside)
    gblock_out[...] = gblock
    branch = gblock.astype(BF16)
    add_up(gw, i, t_dot(merged[...], branch))
    v_large = (large[...] - norm_two[0:1]) * norm_two[1:2]
    v_small = (small[...] - norm_two[2:3]) * norm_two[3:4]
    pre = v_large * gb[2:3] + v_small * gb[3:4] + (gb[7:8] + gb[8:9])
    _, slope = gelu_parts(pre)
    g = here * slope * dot_t(branch, w_out[...])
    g_out[...] = g
    add_up(acc, i, rows_of(down(g), down(g * v_large), down(g * v_small)))

    @pl.when(i == steps - 1)
    def _():
        tell(st_out, acc[...])
        gout_out[...] = gw[...].astype(BF16)


def spread_back_kernel(
    images, st, norm, norm_one, norm_two, gb, mask, inner, large, small, g, moved, fourier, back,
    tap_large, tap_small, waves_large, waves_small, g_out, gk_out, sums_out, st_out,
):
    sums = jnp.sum(st[...], axis=0)
    sums_out[...] = sums
    pixels = norm[2:3]
    by_bias = sums[0:1] / pixels
    half = fourier.shape[0] // 2
    totals = None
    kernel_moved = [None, None]
    for n in range(images):
        rows = slice(n * SPOTS, (n + 1) * SPOTS)
        here = mask[rows]
        sc, ss = moved[n, :half], moved[n, half:]
        total_c = total_s = None
        for k, (value, tap) in enumerate(((large, tap_large), (small, tap_small))):
            average, inverse = norm_two[2 * k : 2 * k + 1], norm_two[2 * k + 1 : 2 * k + 2]
            normal = (value[rows] - average) * inverse
            inside = g[rows] - (by_bias + normal * (sums[1 + k : 2 + k] / pixels))
            gradient = (here * (gb[2 + k : 3 + k] * inverse * inside)).astype(BF16)
            change = dot(fourier[...], gradient)
            gc, gs = change[:half], change[half:]
            kc, ks = tap[:half], tap[half:]
            real, imag = gc * kc - gs * ks, gc * ks + gs * kc
            total_c = real if k == 0 else total_c + real
            total_s = imag if k == 0 else total_s + imag
            real, imag = sc * gc + ss * gs, ss * gc - sc * gs
            pair = kernel_moved[k]
            kernel_moved[k] = (real, imag) if n == 0 else (pair[0] + real, pair[1] + imag)
        both = jnp.concatenate([total_c.astype(BF16), total_s.astype(BF16)], axis=0)
        grad_spread = dot(back[...], both)
        normal = (inner[rows] - norm_one[0:1]) * norm_one[1:2]
        _, slope = gelu_parts(normal * gb[1:2] + gb[6:7])
        first = here * slope * grad_spread
        g_out[rows] = first
        part = rows_of(down(first), down(first * normal))
        totals = part if n == 0 else totals + part
    tell(st_out, totals)
    for k, table in enumerate((waves_large, waves_small)):
        real, imag = kernel_moved[k]
        both = jnp.concatenate([real.astype(BF16), imag.astype(BF16)], axis=0)
        width = waves_large.shape[1]
        place = slice(0, width) if k == 0 else slice(width, width + table.shape[1])
        gk_out[:, place] = t_dot(both, table[...]).astype(BF16)


def give_back(images, i, rel, ratio, target, grad, own, prev):
    @pl.when(i == 0)
    def _():
        prev[...] = jnp.zeros_like(prev)
        own[...] = jnp.zeros_like(own)

    chosen = (target[0] == lax.broadcasted_iota(jnp.int32, (SPOTS, SPOTS), 0)).astype(BF16)
    grad = dot(chosen, grad)
    own[i] += ratio[i] * grad
    giving = (1.0 - ratio[i]) * grad
    to = rel[i]

    @pl.when(to < images)
    def _():
        prev[jnp.minimum(to, images - 1)] += giving

    @pl.when(to >= images)
    def _():
        own[jnp.maximum(to - images, 0)] += giving


def normal_kernel(images, rel, ratio, norm, mask, x, target, own_out, prev_out, own, prev):
    i = pl.program_id(0)
    here = mask[...]
    normal = here * ((x[0] - norm[0:1]) * norm[1:2])
    ones = jnp.broadcast_to(here, (SPOTS, own.shape[2] - normal.shape[1]))
    give_back(images, i, rel, ratio, target, jnp.concatenate([normal, ones], axis=1).astype(BF16), own, prev)

    @pl.when(i == images - 1)
    def _():
        own_out[...] = own[...].astype(BF16)
        prev_out[...] = prev[...].astype(BF16)


def unmix_kernel(
    images, rel, ratio, st, norm, norm_one, gb, mask, inner, g, first, gblock, x, w_in, target,
    own, prev_out, gin_out, sums_out, st_out, prev, coef, acc, gw,
):
    i = pl.program_id(0)

    @pl.when(i == 0)
    def _():
        coef[...] = jnp.sum(st[...], axis=0)
        sums_out[...] = coef[...]

    here = mask[...]
    normal = (inner[0] - norm_one[0:1]) * norm_one[1:2]
    inside = g[0] - (coef[0:1] + normal * coef[1:2]) / norm[2:3]
    grad = (here * (gb[1:2] * norm_one[1:2] * inside)).astype(BF16)
    add_up(gw, i, t_dot(first[0], grad))
    gf = here * dot_t(grad, w_in[...])
    normal = (x[0] - norm[0:1]) * norm[1:2]
    add_up(acc, i, rows_of(down(gf), down(gf * normal)))
    value = (here * gblock[0] + (gb[0:1] * norm[1:2]) * gf).astype(BF16)
    give_back(images, i, rel, ratio, target, value, own, prev)

    @pl.when(i == images - 1)
    def _():
        prev_out[...] = prev[...].astype(BF16)
        gin_out[...] = gw[...].astype(BF16)
        tell(st_out, acc[...])


def finish_kernel(st, norm, gb, own, returned, own_normal, back_normal, out, sums_out):
    sums = jnp.sum(st[...], axis=0)
    sums_out[...] = sums
    channels = own.shape[2]
    factor = gb[0:1] * norm[1:2] / norm[2:3]
    normal = own_normal[0].astype(F32) + back_normal[0].astype(F32)
    less = normal[:, channels : channels + 1] * (factor * sums[0:1]) + normal[:, :channels] * (factor * sums[1:2])
    out[0] = own[0] + returned[0].astype(F32) - less


def shape(dims, kind=F32):
    return jax.ShapeDtypeStruct(dims, kind)


def whole(dims):
    return pl.BlockSpec(dims, lambda *_: (0,) * len(dims))


def by_rows(rows, columns):
    return pl.BlockSpec((rows, columns), lambda i: (i, 0))


def params():
    return pltpu.CompilerParams(vmem_limit_bytes=VMEM)


def shifted(block, distance):
    count = lax.axis_size(BOTH)
    return lax.ppermute(block, BOTH, [((i - distance) % count, i) for i in range(count)])


def exchange(parts):
    return lax.all_to_all(parts, BOTH, 0, 0)


def to_chips(parts):
    return lax.all_to_all(parts, "batch", 0, 0)


def tie(*values):
    return lax.optimization_barrier(values)


def swapped(block):
    return lax.ppermute(block, "hid", [(0, 1), (1, 0)])


def pick(array, index, axis):
    return lax.dynamic_index_in_dim(array, index, axis, keepdims=False)


def added(kept, received, kind=BF16):
    return (kept.astype(F32) + received.astype(F32)).astype(kind)


def split_hid(array):
    count, chips = lax.axis_size(BOTH), lax.axis_size("batch")
    array = array.reshape(chips, count // chips, -1, array.shape[-1])
    mine = lax.axis_index("hid")
    return pick(array, mine, 1), pick(array, 1 - mine, 1)


def chip_bits():
    return lax.axis_size("batch").bit_length() - 1


def flip(bit):
    return [(i, i ^ (1 << bit)) for i in range(lax.axis_size("batch"))]


def by_bits(array):
    return array.reshape((2,) * chip_bits() + array.shape[-2:])


def split_bit(array, bits, bit):
    mine = (lax.axis_index("batch") >> bit) & 1
    axis = bits.index(bit)
    return pick(array, mine, axis), pick(array, 1 - mine, axis)


def send_bit(block, bit):
    return lax.ppermute(block, "batch", flip(bit))


def over_bits(array, bits):
    for bit in reversed(bits):
        kept, sent = split_bit(array, bits, bit)
        bits = [other for other in bits if other != bit]
        array = added(kept, send_bit(sent, bit), BF16 if bits else F32)
    return array


def beside(own, other, low, axis=-3):
    return jnp.stack([jnp.where(low, own, other), jnp.where(low, other, own)], axis=axis)


def beside_bit(own, other, bit, axis=-3):
    return beside(own, other, (lax.axis_index("batch") >> bit) & 1 == 0, axis)


def double(block, bit):
    return beside_bit(block, send_bit(block, bit), bit)


def beside_hid(own, other):
    return beside(own, other, lax.axis_index("hid") == 0).reshape(-1, own.shape[-1])


def shards(
    raw_maps, partner, ratios, offsets, flip_bits, size_class, proj_in, kernel_large, kernel_small,
    proj_out, norm_gain, norm_bias, ffn_up, ffn_down, cotangent,
):
    images, channels = raw_maps.shape[0], raw_maps.shape[3]
    share = proj_in.shape[0]
    count = lax.axis_size(BOTH)
    position = lax.axis_index(BOTH)
    pixels_here = images * SPOTS
    rows = pixels_here // STEPS
    large_extent, small_extent = kernel_large.shape[0], kernel_small.shape[0]
    large_taps, small_taps = large_extent**2, small_extent**2
    large_wide, small_wide = padded(large_taps), padded(small_taps)
    spots = [(r, c) for r in range(CANVAS) for c in range(CANVAS)]
    fourier_np = waves(spots, large_extent, SPOTS, False)
    fourier, back = jnp.asarray(fourier_np), jnp.asarray(np.ascontiguousarray(fourier_np.T))
    waves_large = jnp.asarray(waves(taps(large_extent), large_extent, large_wide, True))
    waves_small = jnp.asarray(waves(taps(small_extent), large_extent, small_wide, True))
    bins = fourier_np.shape[0]

    raw = raw_maps.reshape(images, SPOTS, channels)
    ct = cotangent.reshape(pixels_here, channels)
    earlier = shifted(raw, 1)

    taps_here = jnp.concatenate(
        [
            jnp.pad(kernel_large.reshape(large_taps, share).T, ((0, 0), (0, large_wide - large_taps))),
            jnp.pad(kernel_small.reshape(small_taps, share).T, ((0, 0), (0, small_wide - small_taps))),
        ],
        axis=1,
    )
    hidden_here = ffn_up.shape[1]
    wide = 256 if hidden_here % 256 == 0 else hidden_here
    per_half = hidden_here // wide
    norms = jnp.pad(jnp.concatenate([norm_gain, norm_bias], axis=0).T, ((0, 0), (0, 118)))
    taps_wide = large_wide + small_wide
    taps_wide = large_wide + small_wide
    bits = chip_bits()
    early = jnp.concatenate([taps_here, proj_in, norms], axis=1)
    ffn_here = jnp.stack([ffn_up.reshape(-1, per_half, wide), ffn_down.T.reshape(-1, per_half, wide)], axis=2)
    ffn = jnp.concatenate([ffn_here.reshape(-1, 2 * hidden_here), proj_out.reshape(ffn_up.shape[0], -1)], axis=1)
    for bit in range(bits - 1, 1, -1):
        early = double(early, bit)
    for bit in range(bits - 1, 2, -1):
        ffn = double(ffn, bit)
    earlier, ffn, early = tie(earlier, ffn, early)
    early_sent, ffn_sent = send_bit(early, 1), send_bit(ffn, 2)

    sides = SMALL + (CANVAS - SMALL) * size_class
    spot = lax.broadcasted_iota(jnp.int32, (images, SPOTS), 1)
    row, column = spot // CANVAS, spot % CANVAS
    inside = (row < sides[:, None]) & (column < sides[:, None])
    corner = jnp.minimum(offsets, (CANVAS - sides)[:, None])
    source = column + corner[:, 1:2]
    source = jnp.where(flip_bits[:, None] > 0, CANVAS - 1 - source, source)
    target = jnp.where(inside, (row + corner[:, 0:1]) * CANVAS + source, -1)
    mask = inside.astype(F32).reshape(pixels_here, 1)
    relative = jnp.mod(partner - (position * images - images), count * images)

    def stats(k):
        return shape((count, k, channels)), whole((count, k, channels))

    def call(time, kernel, grid, ins, in_specs, outs, out_specs, scratch=(), prefetch=0):
        cost = pl.CostEstimate(flops=int(time * 1.15e9), bytes_accessed=int(time * 1e6), transcendentals=0)
        spec = pltpu.PrefetchScalarGridSpec(
            num_scalar_prefetch=prefetch, grid=grid, in_specs=in_specs, out_specs=out_specs, scratch_shapes=list(scratch)
        )
        return pl.pallas_call(kernel, grid_spec=spec, out_shape=outs, compiler_params=params(), cost_estimate=cost)(*ins)

    row_c = by_rows(rows, channels)
    row_1 = by_rows(rows, 1)
    map_f = shape((pixels_here, channels))
    map_b = shape((pixels_here, channels), BF16)
    norm_spec = whole((3, channels))
    gb_spec = whole((16, channels))
    square = whole((channels, channels))
    image_spec = pl.BlockSpec((1, SPOTS, channels), lambda i, *_: (i, 0, 0))
    image_f = shape((images, SPOTS, channels))

    shape3, spec3 = stats(3)
    x, st = call(
        6,
        functools.partial(mix_kernel, images),
        (images,),
        (relative, ratios, sides, raw, earlier, raw, target[:, :, None]),
        [
            image_spec,
            pl.BlockSpec((1, SPOTS, channels), lambda i, rel, *_: (jnp.minimum(rel[i], images - 1), 0, 0)),
            pl.BlockSpec((1, SPOTS, channels), lambda i, rel, *_: (jnp.maximum(rel[i] - images, 0), 0, 0)),
            pl.BlockSpec((1, SPOTS, 1), lambda i, *_: (i, 0, 0)),
        ],
        (image_f, shape3),
        (image_spec, spec3),
        [pltpu.VMEM((SPOTS, channels), BF16), pltpu.VMEM((3, channels), F32)],
        prefetch=3,
    )
    x = x.reshape(pixels_here, channels)
    st, x, early, early_sent, ffn = tie(st, x, early, early_sent, ffn)
    early = beside_bit(early, early_sent, 1)
    early = double(early, 0)
    ffn = beside_bit(ffn, ffn_sent, 2)
    st, early, ffn = tie(exchange(st), early, ffn)
    early = beside_hid(early, swapped(early))
    kt, w_in = early[:, :taps_wide], early[:, taps_wide : taps_wide + channels]
    gb = early[:, taps_wide + channels :][:, :16].T.astype(F32)
    ffn_a, ffn_b = ffn[..., :hidden_here], ffn[..., hidden_here:]
    sent_a, sent_b = send_bit(ffn_a, 1), send_bit(ffn_b, 0)

    shape2, spec2 = stats(2)
    first, inner, norm, st = call(
        6,
        functools.partial(inner_kernel, STEPS),
        (STEPS,),
        (st, gb, mask, x, w_in),
        [spec3, gb_spec, row_1, row_c, square],
        (map_b, map_f, shape((3, channels)), shape2),
        (row_c, row_c, norm_spec, spec2),
        [pltpu.VMEM((3, channels), F32), pltpu.VMEM((2, channels), F32)],
    )
    st, first, inner, norm, ffn_a, ffn_b, kt = tie(st, first, inner, norm, ffn_a, ffn_b, kt)
    ffn_a, ffn_b = beside_bit(ffn_a, sent_a, 1), beside_bit(ffn_b, sent_b, 0)

    chunk = 256 if channels % 256 == 0 else channels
    chunks = channels // chunk
    tap_shape = shape((bins, channels))
    tap_spec = pl.BlockSpec((bins, chunk), lambda i: (0, i))
    kt_spec = pl.BlockSpec((chunk, large_wide + small_wide), lambda i: (i, 0))
    wl_spec, ws_spec = whole((bins, large_wide)), whole((bins, small_wide))
    tap_large, tap_small = call(
        5,
        taps_kernel,
        (chunks,),
        (kt, waves_large, waves_small),
        [kt_spec, wl_spec, ws_spec],
        (tap_shape, tap_shape),
        (tap_spec, tap_spec),
    )

    def chunk_stats(k):
        return pl.BlockSpec((count, k, chunk), lambda i: (0, 0, i))

    def chunk_rows(k):
        return pl.BlockSpec((k, chunk), lambda i: (0, i))

    four_spec, back_spec = whole((bins, SPOTS)), whole((SPOTS, bins))
    mask_spec = whole((pixels_here, 1))
    shape4, spec4 = stats(4)
    moved_spec = pl.BlockSpec((images, bins, chunk), lambda i: (0, 0, i))
    st, tap_large, tap_small, ffn_a, ffn_b = tie(exchange(st), tap_large, tap_small, ffn_a, ffn_b)
    sent_a, sent_b = send_bit(ffn_a, 0), send_bit(ffn_b, 1)
    large, small, moved, norm_one, st = call(
        14,
        functools.partial(spread_kernel, images),
        (chunks,),
        (st, norm, gb, mask, inner, fourier, back, tap_large, tap_small),
        [chunk_stats(2), chunk_rows(3), chunk_rows(16), mask_spec, chunk_rows(pixels_here), four_spec, back_spec, tap_spec, tap_spec],
        (map_f, map_f, shape((images, bins, channels)), shape((2, channels)), shape4),
        (chunk_rows(pixels_here), chunk_rows(pixels_here), moved_spec, chunk_rows(2), chunk_stats(4)),
    )
    st, large, small, moved, ffn_a, ffn_b, norm_last = tie(st, large, small, moved, ffn_a, ffn_b, norm)
    ffn_a = beside_bit(ffn_a, sent_a, 0).reshape(channels, -1)
    ffn_b = beside_bit(ffn_b, sent_b, 1, -4).reshape(channels, -1)
    w_out = ffn_b[:, hidden_here:].reshape(-1, share, channels)
    w_out = beside_hid(w_out, swapped(w_out))
    image_f = shape((images, SPOTS, channels))
    target_row = target[:, None, :]
    row_spec = pl.BlockSpec((1, 1, SPOTS), lambda i, *_: (i, 0, 0))
    image_mask = pl.BlockSpec((SPOTS, 1), lambda i, *_: (i, 0))
    broad = (images, SPOTS, channels + 128)
    own_normal, prev_normal = call(
        4,
        functools.partial(normal_kernel, images),
        (images,),
        (relative, ratios, norm_last, mask, x.reshape(images, SPOTS, channels), target_row),
        [norm_spec, image_mask, image_spec, row_spec],
        (shape(broad, BF16), shape(broad, BF16)),
        (whole(broad), whole(broad)),
        [pltpu.VMEM(broad, F32), pltpu.VMEM(broad, F32)],
        prefetch=2,
    )

    st, w_out, ffn_a, ffn_b, prev_normal = tie(exchange(st), w_out, ffn_a, ffn_b, prev_normal)
    other_a, other_b = swapped(ffn_a), swapped(ffn_b[:, :hidden_here])

    merged, block, norm_two, st = call(
        7,
        functools.partial(merge_kernel, STEPS),
        (STEPS,),
        (st, norm, gb, mask, large, small, x, w_out),
        [spec4, norm_spec, gb_spec, row_1, row_c, row_c, row_c, square],
        (map_b, map_f, shape((4, channels)), shape2),
        (row_c, row_c, whole((4, channels)), spec2),
        [pltpu.VMEM((4, channels), F32), pltpu.VMEM((2, channels), F32)],
    )
    st, merged, block, other_a, other_b, prev_normal = tie(exchange(st), merged, block, other_a, other_b, prev_normal)
    back_normal = shifted(prev_normal, -1)

    steps = 2 * per_half
    map_spec = whole((pixels_here, channels))
    own_spec = pl.BlockSpec((channels, 2 * wide), lambda j: (0, jnp.minimum(j, per_half - 1)))
    other_spec = pl.BlockSpec((channels, 2 * wide), lambda j: (0, jnp.maximum(j - per_half, 0)))
    last = per_half // 2 - 1
    quarters = [
        pl.BlockSpec((channels, 2 * wide), lambda j, q=q: (0, jnp.clip(j - q * (last + 1), 0, last))) for q in range(4)
    ]
    gw_shape = shape((channels, 2 * hidden_here), BF16)
    output, gn, norm_four, st, gown, gother = call(
        29,
        functools.partial(ffn_kernel, steps, wide),
        (steps,),
        (st, norm, gb, mask, block, ct, ffn_a, ffn_b, other_a, other_b),
        [spec2, norm_spec, gb_spec, mask_spec, map_spec, map_spec] + quarters,
        (map_b, map_f, shape((2, channels)), shape2, gw_shape, gw_shape),
        (map_spec, map_spec, whole((2, channels)), spec2, own_spec, other_spec),
        [
            pltpu.VMEM((pixels_here, channels), BF16),
            pltpu.VMEM((channels, pixels_here), BF16),
            pltpu.VMEM((channels, pixels_here), BF16),
            pltpu.VMEM((pixels_here, channels), F32),
            pltpu.VMEM((pixels_here, channels), F32),
            pltpu.VMEM((2, channels), F32),
            pltpu.VMEM((channels, 2 * wide), BF16),
            pltpu.VMEM((channels, 2 * wide), BF16),
        ],
    )
    st, output, gn, gown, gother, back_normal = tie(st, output, gn, gown, gother, back_normal)
    gffn = by_bits(added(gown, swapped(gother)).reshape(count // 2, -1, 2 * hidden_here))
    left = list(reversed(range(bits)))
    kept_a, sent_a = split_bit(gffn[..., :hidden_here], left, 0)
    kept_b, sent_b = split_bit(gffn[..., hidden_here:], left, 1)
    st, kept_a, sent_a, kept_b, sent_b = tie(exchange(st), kept_a, sent_a, kept_b, sent_b)
    sent_a, sent_b = send_bit(sent_a, 0), send_bit(sent_b, 1)

    gw_here = shape((channels, channels), BF16)
    gblock, gout, g, sums_four, st = call(
        11,
        functools.partial(merge_back_kernel, STEPS),
        (STEPS,),
        (st, norm, norm_two, norm_four, gb, mask, block, gn, ct, merged, large, small, w_out),
        [spec2, norm_spec, whole((4, channels)), whole((2, channels)), gb_spec, row_1] + [row_c] * 6 + [square],
        (map_f, gw_here, map_f, shape((2, channels)), shape3),
        (row_c, square, row_c, whole((2, channels)), spec3),
        [pltpu.VMEM((2, channels), F32), pltpu.VMEM((3, channels), F32), pltpu.VMEM((channels, channels), F32)],
    )
    st, gblock, gout, g, kept_a, kept_b = tie(st, gblock, gout, g, kept_a, kept_b)
    kept_a, sent_a = split_bit(added(kept_a, sent_a), left[:-1], 1)
    kept_b, sent_b = split_bit(added(kept_b, sent_b), left[:-2] + [0], 0)
    st, kept_a, sent_a, kept_b, sent_b = tie(exchange(st), kept_a, sent_a, kept_b, sent_b)
    sent_a, sent_b = send_bit(sent_a, 1), send_bit(sent_b, 0)

    gk_shape = shape((channels, large_wide + small_wide), BF16)
    map_chunk = chunk_rows(pixels_here)
    g, gk, sums_two, st = call(
        21,
        functools.partial(spread_back_kernel, images),
        (chunks,),
        (st, norm, norm_one, norm_two, gb, mask, inner, large, small, g, moved, fourier, back, tap_large, tap_small, waves_large, waves_small),
        [chunk_stats(3), chunk_rows(3), chunk_rows(2), chunk_rows(4), chunk_rows(16), mask_spec, map_chunk, map_chunk, map_chunk, map_chunk,
         moved_spec, four_spec, back_spec, tap_spec, tap_spec, wl_spec, ws_spec],
        (map_f, gk_shape, shape((3, channels)), shape2),
        (map_chunk, kt_spec, chunk_rows(3), chunk_stats(2)),
    )
    st, gk, g, kept_a, kept_b = tie(st, gk, g, kept_a, kept_b)
    kept, sent = split_hid(jnp.concatenate([gk, gout], axis=1))
    gmiddle = by_bits(added(kept, swapped(sent)))
    kept_m, sent_m = split_bit(gmiddle, left, 0)
    gffn = jnp.concatenate([added(kept_a, sent_a), added(kept_b, sent_b)], axis=-1)
    kept, sent = split_bit(gffn, left[:-2], bits - 1)
    st, kept, sent, kept_m, sent_m = tie(exchange(st), kept, sent, kept_m, sent_m)
    sent, sent_m = send_bit(sent, bits - 1), send_bit(sent_m, 0)

    all_images = whole((images, SPOTS, channels))

    def as_images(array):
        return array.reshape(images, SPOTS, channels)

    own, prev, gin, sums_one, st = call(
        12,
        functools.partial(unmix_kernel, images),
        (images,),
        (
            relative, ratios, st, norm, norm_one, gb, mask, as_images(inner), as_images(g), as_images(first),
            as_images(gblock), as_images(x), w_in, target_row,
        ),
        [spec2, norm_spec, whole((2, channels)), gb_spec, image_mask] + [image_spec] * 5 + [square, row_spec],
        (image_f, shape((images, SPOTS, channels), BF16), gw_here, shape((2, channels)), shape2),
        (all_images, all_images, square, whole((2, channels)), spec2),
        [
            pltpu.VMEM((images, SPOTS, channels), F32),
            pltpu.VMEM((2, channels), F32),
            pltpu.VMEM((2, channels), F32),
            pltpu.VMEM((channels, channels), F32),
        ],
        prefetch=2,
    )
    st, own, prev, gin, kept, kept_m = tie(st, own, prev, gin, kept, kept_m)
    returned = shifted(prev, -1)
    kept_in, sent_in = split_hid(gin)
    gin = added(kept_in, swapped(sent_in))
    gmiddle = added(kept_m, sent_m)
    gffn = added(kept, sent)
    st, gin, gmiddle, gffn = tie(exchange(st), gin, gmiddle, gffn)
    gmiddle = over_bits(gmiddle, left[:-1])
    gffn = over_bits(gffn, left[1:-2])
    gin = jnp.sum(to_chips(gin).astype(F32), axis=0)
    broad_spec = pl.BlockSpec((1,) + broad[1:], lambda i: (i, 0, 0))
    one_image = pl.BlockSpec((1, SPOTS, channels), lambda i: (i, 0, 0))
    grad_raw, sums_zero = call(
        4,
        finish_kernel,
        (images,),
        (st, norm, gb, own, returned, own_normal, back_normal),
        [spec2, norm_spec, gb_spec, one_image, one_image, broad_spec, broad_spec],
        (image_f, shape((2, channels))),
        (one_image, whole((2, channels))),
    )

    gains = jnp.concatenate([sums_zero[1:2], sums_one[1:2], sums_two[1:3], sums_four[1:2]], axis=0)
    biases = jnp.concatenate([sums_zero[0:1], sums_one[0:1], sums_two[0:1], sums_two[0:1], sums_four[0:1]], axis=0)
    gffn = gffn.reshape(-1, per_half, 2, wide)
    canvas = (images, CANVAS, CANVAS, channels)
    return (
        output.reshape(canvas),
        grad_raw.reshape(canvas),
        gin,
        gmiddle[:, :large_taps].T.reshape(large_extent, large_extent, share),
        gmiddle[:, large_wide : large_wide + small_taps].T.reshape(small_extent, small_extent, share),
        gmiddle[:, taps_wide : taps_wide + channels],
        lax.dynamic_slice_in_dim(gains, position * share, share, 1),
        lax.dynamic_slice_in_dim(biases, position * share, share, 1),
        gffn[:, :, 0].reshape(-1, hidden_here),
        gffn[:, :, 1].reshape(-1, hidden_here).T,
    )


def solution(mesh):
    one = P(BOTH)
    maps = P(BOTH, None, None, None)
    flat = P(BOTH, None)
    kernels = P(None, None, BOTH)
    norms = P(None, BOTH)
    return jax.shard_map(
        shards,
        mesh=mesh,
        in_specs=(
            maps, one, one, flat, one, one, flat, kernels, kernels, flat, norms, norms,
            P("batch", "hid"), P("hid", "batch"), maps,
        ),
        out_specs=(maps, maps, flat, kernels, kernels, flat, norms, norms, P("batch", "hid"), P("hid", "batch")),
        check_vma=False,
    )
```

```python
import functools

import jax
import jax.numpy as jnp
import ml_dtypes
import numpy as np
from jax import lax
from jax.experimental import pallas as pl
from jax.experimental.pallas import tpu as pltpu
from jax.sharding import PartitionSpec as P

CANVAS = 24
SMALL = 14
SPOTS = CANVAS * CANVAS
EPS = 1e-05
BOTH = ("batch", "hid")
ROOT = float(np.sqrt(2.0 / np.pi))
CUBE = 0.044715
F32 = jnp.float32
BF16 = jnp.bfloat16
STEPS = 2
VMEM = 56 * 1024 * 1024


def frequencies(extent):
    side = CANVAS + (extent - 1) // 2
    half = [(0, v) for v in range(side // 2 + 1)]
    half += [(u, v) for u in range(1, side // 2 + 1) for v in range(side)]
    if side % 2 == 0:
        raise ValueError("even side")
    return side, np.array(half, np.float64)


def waves(points, extent, columns, scaled):
    side, half = frequencies(extent)
    count = -(-len(half) // 16) * 16
    angle = 2.0 * np.pi / side * (half @ np.array(points, np.float64).T)
    weight = np.where(np.arange(len(half)) == 0, 1.0, 2.0)[:, None] / side**2 if scaled else 1.0
    table = np.zeros((2 * count, columns), np.float64)
    table[: len(half), : len(points)] = np.cos(angle) * weight
    table[count : count + len(half), : len(points)] = np.sin(angle) * weight
    return table.astype(ml_dtypes.bfloat16)


def taps(extent):
    radius = (extent - 1) // 2
    return [(a - radius, b - radius) for a in range(extent) for b in range(extent)]


def padded(count):
    return -(-count // 128) * 128


def dot(a, b):
    return lax.dot_general(a, b, (((1,), (0,)), ((), ())), preferred_element_type=F32)


def dot_t(a, b):
    return lax.dot_general(a, b, (((1,), (1,)), ((), ())), preferred_element_type=F32)


def t_dot(a, b):
    return lax.dot_general(a, b, (((0,), (0,)), ((), ())), preferred_element_type=F32)


def gelu_parts(v):
    square = v * v
    bend = jnp.tanh(ROOT * v * (1.0 + CUBE * square))
    half = 0.5 + 0.5 * bend
    slope = half + (0.5 * ROOT) * v * (1.0 - bend * bend) * (1.0 + (3.0 * CUBE) * square)
    return v * half, slope


def gelu(v):
    return v * (0.5 + 0.5 * jnp.tanh(ROOT * v * (1.0 + CUBE * v * v)))


def center(totals, squares, pixels):
    average = totals / pixels
    return average, lax.rsqrt(squares / pixels - average * average + EPS)


def rows_of(*rows):
    return jnp.concatenate(rows, axis=0)


def down(v):
    return jnp.sum(v, axis=0, keepdims=True)


def tell(ref, rows):
    ref[...] = jnp.broadcast_to(rows[None], ref.shape)


def add_up(acc, step, rows):
    @pl.when(step == 0)
    def _():
        acc[...] = rows

    @pl.when(step > 0)
    def _():
        acc[...] += rows


def mix_kernel(images, rel, ratio, sides, own, first, second, target, x_out, st_out, other, acc):
    i = pl.program_id(0)

    @pl.when(rel[i] < images)
    def _():
        other[...] = first[0]

    @pl.when(rel[i] >= images)
    def _():
        other[...] = second[0]

    pick = (target[0] == lax.broadcasted_iota(jnp.int32, (SPOTS, SPOTS), 1)).astype(BF16)
    x = ratio[i] * dot(pick, own[0]) + (1.0 - ratio[i]) * dot(pick, other[...])
    x_out[0] = x
    pixels = jnp.full((1, x.shape[1]), (sides[i] * sides[i]).astype(F32), F32)
    add_up(acc, i, rows_of(down(x), down(x * x), pixels))

    @pl.when(i == images - 1)
    def _():
        tell(st_out, acc[...])


def inner_kernel(steps, st, gb, mask, x, w_in, first_out, inner_out, norm_out, st_out, coef, acc):
    i = pl.program_id(0)

    @pl.when(i == 0)
    def _():
        sums = jnp.sum(st[...], axis=0)
        pixels = sums[2:3]
        average, inverse = center(sums[0:1], sums[1:2], pixels)
        coef[...] = rows_of(average, inverse, pixels)
        norm_out[...] = coef[...]

    scale = coef[1:2] * gb[0:1]
    shift = gb[5:6] - coef[0:1] * scale
    first = ((x[...] * scale + shift) * mask[...]).astype(BF16)
    first_out[...] = first
    inner = dot(first, w_in[...])
    inner_out[...] = inner
    inner = inner * mask[...]
    add_up(acc, i, rows_of(down(inner), down(inner * inner)))

    @pl.when(i == steps - 1)
    def _():
        tell(st_out, acc[...])


def taps_kernel(kt, waves_large, waves_small, large_out, small_out):
    large = waves_large.shape[1]
    large_out[...] = dot_t(waves_large[...], kt[:, :large])
    small_out[...] = dot_t(waves_small[...], kt[:, large:])


def spread_kernel(
    images, st, norm, gb, mask, inner, fourier, back, tap_large, tap_small,
    large_out, small_out, moved_out, norm_out, st_out,
):
    sums = jnp.sum(st[...], axis=0)
    pixels = norm[2:3]
    average, inverse = center(sums[0:1], sums[1:2], pixels)
    norm_out[...] = rows_of(average, inverse)
    scale = inverse * gb[1:2]
    shift = gb[6:7] - average * scale
    half = fourier.shape[0] // 2
    totals = None
    for n in range(images):
        rows = slice(n * SPOTS, (n + 1) * SPOTS)
        here = mask[rows]
        spread = (gelu(inner[rows] * scale + shift) * here).astype(BF16)
        moved = dot(fourier[...], spread)
        moved_out[n] = moved
        mc, ms = moved[:half], moved[half:]
        outs = []
        for tap in (tap_large, tap_small):
            kc, ks = tap[:half], tap[half:]
            both = jnp.concatenate(
                [(mc * kc + ms * ks).astype(BF16), (ms * kc - mc * ks).astype(BF16)], axis=0
            )
            outs.append(dot(back[...], both))
        large_out[rows] = outs[0]
        small_out[rows] = outs[1]
        large, small = outs[0] * here, outs[1] * here
        part = rows_of(down(large), down(large * large), down(small), down(small * small))
        totals = part if totals is None else totals + part
    tell(st_out, totals)


def merge_kernel(steps, st, norm, gb, mask, large, small, x, w_out, merged_out, block_out, norm_out, st_out, coef, acc):
    i = pl.program_id(0)

    @pl.when(i == 0)
    def _():
        sums = jnp.sum(st[...], axis=0)
        pixels = norm[2:3]
        coef[...] = rows_of(*center(sums[0:1], sums[1:2], pixels), *center(sums[2:3], sums[3:4], pixels))
        norm_out[...] = coef[...]

    by_large = coef[1:2] * gb[2:3]
    by_small = coef[3:4] * gb[3:4]
    shift = gb[7:8] + gb[8:9] - coef[0:1] * by_large - coef[2:3] * by_small
    pre = large[...] * by_large + small[...] * by_small + shift
    merged = (gelu(pre) * mask[...]).astype(BF16)
    merged_out[...] = merged
    block = x[...] + dot(merged, w_out[...])
    block_out[...] = block
    block = block * mask[...]
    add_up(acc, i, rows_of(down(block), down(block * block)))

    @pl.when(i == steps - 1)
    def _():
        tell(st_out, acc[...])


def ffn_kernel(
    steps, wide, st, norm, gb, mask, block, ct, own_a, own_b, other_a, other_b,
    out, gn_out, norm_out, st_out, gown_out, gother_out,
    normed, normed_t, ct_t, branch, gn, coef, w, gw,
):
    j = pl.program_id(0)

    @pl.when(j == 0)
    def _():
        sums = jnp.sum(st[...], axis=0)
        coef[...] = rows_of(*center(sums[0:1], sums[1:2], norm[2:3]))
        norm_out[...] = coef[...]
        scale = coef[1:2] * gb[4:5]
        shift = gb[9:10] - coef[0:1] * scale
        value = ((block[...] * scale + shift) * mask[...]).astype(BF16)
        normed[...] = value
        normed_t[...] = value.T
        ct_t[...] = ct[...].T
        branch[...] = jnp.zeros_like(branch)
        gn[...] = jnp.zeros_like(gn)

    for quarter, part in enumerate((own_a, own_b, other_a, other_b)):

        @pl.when(j // (steps // 4) == quarter)
        def _():
            w[...] = part[...]

    up, dn = w[:, :wide], w[:, wide:]
    hidden, slope = gelu_parts(dot(normed[...], up))
    hidden = hidden.astype(BF16)
    branch[...] += dot_t(hidden, dn)
    gw[:, wide:] = dot(ct_t[...], hidden).astype(BF16)
    grad = (slope * dot(ct[...], dn)).astype(BF16)
    gw[:, :wide] = dot(normed_t[...], grad).astype(BF16)
    gn[...] += dot_t(grad, up)

    @pl.when(j < steps // 2)
    def _():
        gown_out[...] = gw[...]

    @pl.when(j >= steps // 2)
    def _():
        gother_out[...] = gw[...]

    @pl.when(j == steps - 1)
    def _():
        out[...] = (block[...] + branch[...]).astype(BF16)
        masked = gn[...] * mask[...]
        gn_out[...] = masked
        normal = (block[...] - coef[0:1]) * coef[1:2]
        tell(st_out, rows_of(down(masked), down(masked * normal)))


def merge_back_kernel(
    steps, st, norm, norm_two, norm_four, gb, mask, block, gn, ct, merged, large, small, w_out,
    gblock_out, gout_out, g_out, sums_out, st_out, coef, acc, gw,
):
    i = pl.program_id(0)

    @pl.when(i == 0)
    def _():
        coef[...] = jnp.sum(st[...], axis=0)
        sums_out[...] = coef[...]

    average, inverse = norm_four[0:1], norm_four[1:2]
    normal = (block[...] - average) * inverse
    here = mask[...]
    inside = gn[...] - (coef[0:1] + normal * coef[1:2]) / norm[2:3]
    gblock = ct[...].astype(F32) + here * (gb[4:5] * inverse * inside)
    gblock_out[...] = gblock
    branch = gblock.astype(BF16)
    add_up(gw, i, t_dot(merged[...], branch))
    v_large = (large[...] - norm_two[0:1]) * norm_two[1:2]
    v_small = (small[...] - norm_two[2:3]) * norm_two[3:4]
    pre = v_large * gb[2:3] + v_small * gb[3:4] + (gb[7:8] + gb[8:9])
    _, slope = gelu_parts(pre)
    g = here * slope * dot_t(branch, w_out[...])
    g_out[...] = g
    add_up(acc, i, rows_of(down(g), down(g * v_large), down(g * v_small)))

    @pl.when(i == steps - 1)
    def _():
        tell(st_out, acc[...])
        gout_out[...] = gw[...].astype(BF16)


def spread_back_kernel(
    images, st, norm, norm_one, norm_two, gb, mask, inner, large, small, g, moved, fourier, back,
    tap_large, tap_small, waves_large, waves_small, g_out, gk_out, sums_out, st_out,
):
    sums = jnp.sum(st[...], axis=0)
    sums_out[...] = sums
    pixels = norm[2:3]
    by_bias = sums[0:1] / pixels
    half = fourier.shape[0] // 2
    totals = None
    kernel_moved = [None, None]
    for n in range(images):
        rows = slice(n * SPOTS, (n + 1) * SPOTS)
        here = mask[rows]
        sc, ss = moved[n, :half], moved[n, half:]
        total_c = total_s = None
        for k, (value, tap) in enumerate(((large, tap_large), (small, tap_small))):
            average, inverse = norm_two[2 * k : 2 * k + 1], norm_two[2 * k + 1 : 2 * k + 2]
            normal = (value[rows] - average) * inverse
            inside = g[rows] - (by_bias + normal * (sums[1 + k : 2 + k] / pixels))
            gradient = (here * (gb[2 + k : 3 + k] * inverse * inside)).astype(BF16)
            change = dot(fourier[...], gradient)
            gc, gs = change[:half], change[half:]
            kc, ks = tap[:half], tap[half:]
            real, imag = gc * kc - gs * ks, gc * ks + gs * kc
            total_c = real if k == 0 else total_c + real
            total_s = imag if k == 0 else total_s + imag
            real, imag = sc * gc + ss * gs, ss * gc - sc * gs
            pair = kernel_moved[k]
            kernel_moved[k] = (real, imag) if n == 0 else (pair[0] + real, pair[1] + imag)
        both = jnp.concatenate([total_c.astype(BF16), total_s.astype(BF16)], axis=0)
        grad_spread = dot(back[...], both)
        normal = (inner[rows] - norm_one[0:1]) * norm_one[1:2]
        _, slope = gelu_parts(normal * gb[1:2] + gb[6:7])
        first = here * slope * grad_spread
        g_out[rows] = first
        part = rows_of(down(first), down(first * normal))
        totals = part if n == 0 else totals + part
    tell(st_out, totals)
    for k, table in enumerate((waves_large, waves_small)):
        real, imag = kernel_moved[k]
        both = jnp.concatenate([real.astype(BF16), imag.astype(BF16)], axis=0)
        width = waves_large.shape[1]
        place = slice(0, width) if k == 0 else slice(width, width + table.shape[1])
        gk_out[:, place] = t_dot(both, table[...]).astype(BF16)


def give_back(images, i, rel, ratio, target, grad, own, prev):
    @pl.when(i == 0)
    def _():
        prev[...] = jnp.zeros_like(prev)
        own[...] = jnp.zeros_like(own)

    chosen = (target[0] == lax.broadcasted_iota(jnp.int32, (SPOTS, SPOTS), 0)).astype(BF16)
    grad = dot(chosen, grad)
    own[i] += ratio[i] * grad
    giving = (1.0 - ratio[i]) * grad
    to = rel[i]

    @pl.when(to < images)
    def _():
        prev[jnp.minimum(to, images - 1)] += giving

    @pl.when(to >= images)
    def _():
        own[jnp.maximum(to - images, 0)] += giving


def normal_kernel(images, rel, ratio, norm, mask, x, target, own_out, prev_out, own, prev):
    i = pl.program_id(0)
    here = mask[...]
    normal = here * ((x[0] - norm[0:1]) * norm[1:2])
    ones = jnp.broadcast_to(here, (SPOTS, own.shape[2] - normal.shape[1]))
    give_back(images, i, rel, ratio, target, jnp.concatenate([normal, ones], axis=1).astype(BF16), own, prev)

    @pl.when(i == images - 1)
    def _():
        own_out[...] = own[...].astype(BF16)
        prev_out[...] = prev[...].astype(BF16)


def in_three(rows):
    parts = []
    for _ in range(3):
        part = rows.astype(BF16)
        parts.append(part)
        rows = rows - part.astype(F32)
    return jnp.concatenate(parts, axis=0)


def unmix_kernel(
    images, rel, ratio, st, norm, norm_one, gb, mask, inner, g, first, gblock, x, w_in, target,
    own, prev_out, gin_out, sums_out, st_out, prev, coef, acc, gw,
):
    i = pl.program_id(0)

    @pl.when(i == 0)
    def _():
        coef[...] = jnp.sum(st[...], axis=0)
        sums_out[...] = coef[...]

    here = mask[...]
    normal = (inner[0] - norm_one[0:1]) * norm_one[1:2]
    inside = g[0] - (coef[0:1] + normal * coef[1:2]) / norm[2:3]
    grad = (here * (gb[1:2] * norm_one[1:2] * inside)).astype(BF16)
    add_up(gw, i, t_dot(first[0], grad))
    gf = here * dot_t(grad, w_in[...])
    normal = (x[0] - norm[0:1]) * norm[1:2]
    add_up(acc, i, rows_of(down(gf), down(gf * normal)))
    value = (here * gblock[0] + (gb[0:1] * norm[1:2]) * gf).astype(BF16)
    give_back(images, i, rel, ratio, target, value, own, prev)

    @pl.when(i == images - 1)
    def _():
        prev_out[...] = prev[...].astype(BF16)
        gin_out[...] = gw[...].astype(BF16)
        tell(st_out, in_three(acc[...]))


def returned_kernel(own, returned, out):
    out[...] = own[...] + returned[...].astype(F32)


def finish_kernel(st, norm, gb, given, own_normal, back_normal, out, sums_out):
    sums = jnp.sum(st[...], axis=0)
    sums_out[...] = sums
    channels = given.shape[2]
    factor = gb[0:1] * norm[1:2] / norm[2:3]
    normal = own_normal[0].astype(F32) + back_normal[0].astype(F32)
    less = normal[:, channels : channels + 1] * (factor * sums[0:1]) + normal[:, :channels] * (factor * sums[1:2])
    out[0] = given[0] - less


def shape(dims, kind=F32):
    return jax.ShapeDtypeStruct(dims, kind)


def whole(dims):
    return pl.BlockSpec(dims, lambda *_: (0,) * len(dims))


def by_rows(rows, columns):
    return pl.BlockSpec((rows, columns), lambda i: (i, 0))


def params():
    return pltpu.CompilerParams(vmem_limit_bytes=VMEM)


def shifted(block, distance):
    count = lax.axis_size(BOTH)
    return lax.ppermute(block, BOTH, [((i - distance) % count, i) for i in range(count)])


def exchange(parts):
    return lax.all_to_all(parts, BOTH, 0, 0)


def to_chips(parts):
    return lax.all_to_all(parts, "batch", 0, 0)


def tie(*values):
    return lax.optimization_barrier(values)


def swapped(block):
    return lax.ppermute(block, "hid", [(0, 1), (1, 0)])


def pick(array, index, axis):
    return lax.dynamic_index_in_dim(array, index, axis, keepdims=False)


def added(kept, received, kind=BF16):
    return (kept.astype(F32) + received.astype(F32)).astype(kind)


def split_hid(array):
    count, chips = lax.axis_size(BOTH), lax.axis_size("batch")
    array = array.reshape(chips, count // chips, -1, array.shape[-1])
    mine = lax.axis_index("hid")
    return pick(array, mine, 1), pick(array, 1 - mine, 1)


def chip_bits():
    return lax.axis_size("batch").bit_length() - 1


def flip(bit):
    return [(i, i ^ (1 << bit)) for i in range(lax.axis_size("batch"))]


def by_bits(array):
    return array.reshape((2,) * chip_bits() + array.shape[-2:])


def split_bit(array, bits, bit):
    mine = (lax.axis_index("batch") >> bit) & 1
    axis = bits.index(bit)
    return pick(array, mine, axis), pick(array, 1 - mine, axis)


def bit_groups():
    left = list(reversed(range(chip_bits())))
    groups = []
    while left:
        size = 1 if len(left) % 2 else 2
        groups.append(left[:size])
        left = left[size:]
    return groups


def moves(group):
    chips = lax.axis_size("batch")
    low = group[-1]
    return [[(i, i ^ (way << low)) for i in range(chips)] for way in range(1, 1 << len(group))]


def field(group):
    return (lax.axis_index("batch") >> group[-1]) & ((1 << len(group)) - 1)


def send_all(block, group):
    return [lax.ppermute(block, "batch", pairs) for pairs in moves(group)]


def beside_all(own, received, group):
    parts = [own, *received]
    mine = field(group)
    for level in range(len(group)):
        flipped = (mine >> level) & 1 == 1
        parts = [jnp.where(flipped, parts[k ^ (1 << level)], parts[k]) for k in range(len(parts))]
    return jnp.stack(parts, axis=-3)


def split_all(array, group):
    mine = field(group)
    return [pick(array, mine ^ way, 0) for way in range(1 << len(group))]


def send_each(parts, group):
    return [lax.ppermute(part, "batch", pairs) for part, pairs in zip(parts, moves(group))]


def send_bit(block, bit):
    return lax.ppermute(block, "batch", flip(bit))


def beside(own, other, low, axis=-3):
    return jnp.stack([jnp.where(low, own, other), jnp.where(low, other, own)], axis=axis)


def beside_bit(own, other, bit, axis=-3):
    return beside(own, other, (lax.axis_index("batch") >> bit) & 1 == 0, axis)


def beside_hid(own, other):
    return beside(own, other, lax.axis_index("hid") == 0).reshape(-1, own.shape[-1])


def shards(
    raw_maps, partner, ratios, offsets, flip_bits, size_class, proj_in, kernel_large, kernel_small,
    proj_out, norm_gain, norm_bias, ffn_up, ffn_down, cotangent,
):
    images, channels = raw_maps.shape[0], raw_maps.shape[3]
    share = proj_in.shape[0]
    count = lax.axis_size(BOTH)
    position = lax.axis_index(BOTH)
    pixels_here = images * SPOTS
    rows = pixels_here // STEPS
    large_extent, small_extent = kernel_large.shape[0], kernel_small.shape[0]
    large_taps, small_taps = large_extent**2, small_extent**2
    large_wide, small_wide = padded(large_taps), padded(small_taps)
    spots = [(r, c) for r in range(CANVAS) for c in range(CANVAS)]
    fourier_np = waves(spots, large_extent, SPOTS, False)
    fourier, back = jnp.asarray(fourier_np), jnp.asarray(np.ascontiguousarray(fourier_np.T))
    waves_large = jnp.asarray(waves(taps(large_extent), large_extent, large_wide, True))
    waves_small = jnp.asarray(waves(taps(small_extent), large_extent, small_wide, True))
    bins = fourier_np.shape[0]

    raw = raw_maps.reshape(images, SPOTS, channels)
    ct = cotangent.reshape(pixels_here, channels)
    earlier = shifted(raw, 1)

    taps_here = jnp.concatenate(
        [
            jnp.pad(kernel_large.reshape(large_taps, share).T, ((0, 0), (0, large_wide - large_taps))),
            jnp.pad(kernel_small.reshape(small_taps, share).T, ((0, 0), (0, small_wide - small_taps))),
        ],
        axis=1,
    )
    hidden_here = ffn_up.shape[1]
    wide = 512 if hidden_here % 512 == 0 else hidden_here
    per_half = hidden_here // wide
    norms = jnp.pad(jnp.concatenate([norm_gain, norm_bias], axis=0).T, ((0, 0), (0, 118)))
    taps_wide = large_wide + small_wide
    taps_wide = large_wide + small_wide
    bits = chip_bits()
    early = jnp.concatenate([taps_here, proj_in, norms], axis=1)
    ffn_here = jnp.stack([ffn_up.reshape(-1, per_half, wide), ffn_down.T.reshape(-1, per_half, wide)], axis=2)
    ffn = jnp.concatenate([ffn_here.reshape(-1, 2 * hidden_here), proj_out.reshape(ffn_up.shape[0], -1)], axis=1)
    groups = bit_groups()
    for group in groups[:-1]:
        early = beside_all(early, send_all(early, group), group)
    earlier, ffn, early = tie(earlier, ffn, early)
    early_sent, ffn_sent = send_all(early, groups[-1]), send_all(ffn, groups[0])

    sides = SMALL + (CANVAS - SMALL) * size_class
    spot = lax.broadcasted_iota(jnp.int32, (images, SPOTS), 1)
    row, column = spot // CANVAS, spot % CANVAS
    inside = (row < sides[:, None]) & (column < sides[:, None])
    corner = jnp.minimum(offsets, (CANVAS - sides)[:, None])
    source = column + corner[:, 1:2]
    source = jnp.where(flip_bits[:, None] > 0, CANVAS - 1 - source, source)
    target = jnp.where(inside, (row + corner[:, 0:1]) * CANVAS + source, -1)
    mask = inside.astype(F32).reshape(pixels_here, 1)
    relative = jnp.mod(partner - (position * images - images), count * images)

    def stats(k):
        return shape((count, k, channels)), whole((count, k, channels))

    def call(time, kernel, grid, ins, in_specs, outs, out_specs, scratch=(), prefetch=0):
        cost = pl.CostEstimate(flops=int(time * 1.15e9), bytes_accessed=int(time * 1e6), transcendentals=0)
        spec = pltpu.PrefetchScalarGridSpec(
            num_scalar_prefetch=prefetch, grid=grid, in_specs=in_specs, out_specs=out_specs, scratch_shapes=list(scratch)
        )
        return pl.pallas_call(kernel, grid_spec=spec, out_shape=outs, compiler_params=params(), cost_estimate=cost)(*ins)

    row_c = by_rows(rows, channels)
    row_1 = by_rows(rows, 1)
    map_f = shape((pixels_here, channels))
    map_b = shape((pixels_here, channels), BF16)
    norm_spec = whole((3, channels))
    gb_spec = whole((16, channels))
    square = whole((channels, channels))
    image_spec = pl.BlockSpec((1, SPOTS, channels), lambda i, *_: (i, 0, 0))
    image_f = shape((images, SPOTS, channels))

    shape3, spec3 = stats(3)
    x, st = call(
        6,
        functools.partial(mix_kernel, images),
        (images,),
        (relative, ratios, sides, raw, earlier, raw, target[:, :, None]),
        [
            image_spec,
            pl.BlockSpec((1, SPOTS, channels), lambda i, rel, *_: (jnp.minimum(rel[i], images - 1), 0, 0)),
            pl.BlockSpec((1, SPOTS, channels), lambda i, rel, *_: (jnp.maximum(rel[i] - images, 0), 0, 0)),
            pl.BlockSpec((1, SPOTS, 1), lambda i, *_: (i, 0, 0)),
        ],
        (image_f, shape3),
        (image_spec, spec3),
        [pltpu.VMEM((SPOTS, channels), BF16), pltpu.VMEM((3, channels), F32)],
        prefetch=3,
    )
    x = x.reshape(pixels_here, channels)
    st, x, early, ffn = tie(st, x, early, ffn)
    early = beside_all(early, early_sent, groups[-1])
    early = beside_hid(early, swapped(early))
    ffn = beside_all(ffn, ffn_sent, groups[0])
    for group in groups[1:-1]:
        ffn = beside_all(ffn, send_all(ffn, group), group)
    st, ffn = tie(exchange(st), ffn)
    kt, w_in = early[:, :taps_wide], early[:, taps_wide : taps_wide + channels]
    gb = early[:, taps_wide + channels :][:, :16].T.astype(F32)
    ffn_a, ffn_b = ffn[..., :hidden_here], ffn[..., hidden_here:]
    sent_a, sent_b = send_bit(ffn_a, 1), send_bit(ffn_b, 0)

    shape2, spec2 = stats(2)
    first, inner, norm, st = call(
        6,
        functools.partial(inner_kernel, STEPS),
        (STEPS,),
        (st, gb, mask, x, w_in),
        [spec3, gb_spec, row_1, row_c, square],
        (map_b, map_f, shape((3, channels)), shape2),
        (row_c, row_c, norm_spec, spec2),
        [pltpu.VMEM((3, channels), F32), pltpu.VMEM((2, channels), F32)],
    )
    st, first, inner, norm, ffn_a, ffn_b, kt = tie(st, first, inner, norm, ffn_a, ffn_b, kt)
    ffn_a, ffn_b = beside_bit(ffn_a, sent_a, 1), beside_bit(ffn_b, sent_b, 0)

    chunk = 256 if channels % 256 == 0 else channels
    chunks = channels // chunk
    tap_shape = shape((bins, channels))
    tap_spec = pl.BlockSpec((bins, chunk), lambda i: (0, i))
    kt_spec = pl.BlockSpec((chunk, large_wide + small_wide), lambda i: (i, 0))
    wl_spec, ws_spec = whole((bins, large_wide)), whole((bins, small_wide))
    tap_large, tap_small = call(
        5,
        taps_kernel,
        (chunks,),
        (kt, waves_large, waves_small),
        [kt_spec, wl_spec, ws_spec],
        (tap_shape, tap_shape),
        (tap_spec, tap_spec),
    )

    def chunk_stats(k):
        return pl.BlockSpec((count, k, chunk), lambda i: (0, 0, i))

    def chunk_rows(k):
        return pl.BlockSpec((k, chunk), lambda i: (0, i))

    four_spec, back_spec = whole((bins, SPOTS)), whole((SPOTS, bins))
    mask_spec = whole((pixels_here, 1))
    shape4, spec4 = stats(4)
    moved_spec = pl.BlockSpec((images, bins, chunk), lambda i: (0, 0, i))
    st, tap_large, tap_small, ffn_a, ffn_b = tie(exchange(st), tap_large, tap_small, ffn_a, ffn_b)
    sent_a, sent_b = send_bit(ffn_a, 0), send_bit(ffn_b, 1)
    large, small, moved, norm_one, st = call(
        14,
        functools.partial(spread_kernel, images),
        (chunks,),
        (st, norm, gb, mask, inner, fourier, back, tap_large, tap_small),
        [chunk_stats(2), chunk_rows(3), chunk_rows(16), mask_spec, chunk_rows(pixels_here), four_spec, back_spec, tap_spec, tap_spec],
        (map_f, map_f, shape((images, bins, channels)), shape((2, channels)), shape4),
        (chunk_rows(pixels_here), chunk_rows(pixels_here), moved_spec, chunk_rows(2), chunk_stats(4)),
    )
    st, large, small, moved, ffn_a, ffn_b, norm_last = tie(st, large, small, moved, ffn_a, ffn_b, norm)
    ffn_a = beside_bit(ffn_a, sent_a, 0).reshape(channels, -1)
    ffn_b = beside_bit(ffn_b, sent_b, 1, -4).reshape(channels, -1)
    w_out = ffn_b[:, hidden_here:].reshape(-1, share, channels)
    w_out = beside_hid(w_out, swapped(w_out))
    image_f = shape((images, SPOTS, channels))
    target_row = target[:, None, :]
    row_spec = pl.BlockSpec((1, 1, SPOTS), lambda i, *_: (i, 0, 0))
    image_mask = pl.BlockSpec((SPOTS, 1), lambda i, *_: (i, 0))
    broad = (images, SPOTS, channels + 128)
    own_normal, prev_normal = call(
        4,
        functools.partial(normal_kernel, images),
        (images,),
        (relative, ratios, norm_last, mask, x.reshape(images, SPOTS, channels), target_row),
        [norm_spec, image_mask, image_spec, row_spec],
        (shape(broad, BF16), shape(broad, BF16)),
        (whole(broad), whole(broad)),
        [pltpu.VMEM(broad, F32), pltpu.VMEM(broad, F32)],
        prefetch=2,
    )

    st, w_out, ffn_a, ffn_b, prev_normal = tie(exchange(st), w_out, ffn_a, ffn_b, prev_normal)
    other_a, other_b = swapped(ffn_a), swapped(ffn_b[:, :hidden_here])

    merged, block, norm_two, st = call(
        7,
        functools.partial(merge_kernel, STEPS),
        (STEPS,),
        (st, norm, gb, mask, large, small, x, w_out),
        [spec4, norm_spec, gb_spec, row_1, row_c, row_c, row_c, square],
        (map_b, map_f, shape((4, channels)), shape2),
        (row_c, row_c, whole((4, channels)), spec2),
        [pltpu.VMEM((4, channels), F32), pltpu.VMEM((2, channels), F32)],
    )
    st, merged, block, other_a, other_b, prev_normal = tie(exchange(st), merged, block, other_a, other_b, prev_normal)
    back_normal = shifted(prev_normal, -1)

    steps = 2 * per_half
    map_spec = whole((pixels_here, channels))
    own_spec = pl.BlockSpec((channels, 2 * wide), lambda j: (0, jnp.minimum(j, per_half - 1)))
    other_spec = pl.BlockSpec((channels, 2 * wide), lambda j: (0, jnp.maximum(j - per_half, 0)))
    last = per_half // 2 - 1
    quarters = [
        pl.BlockSpec((channels, 2 * wide), lambda j, q=q: (0, jnp.clip(j - q * (last + 1), 0, last))) for q in range(4)
    ]
    gw_shape = shape((channels, 2 * hidden_here), BF16)
    output, gn, norm_four, st, gown, gother = call(
        29,
        functools.partial(ffn_kernel, steps, wide),
        (steps,),
        (st, norm, gb, mask, block, ct, ffn_a, ffn_b, other_a, other_b),
        [spec2, norm_spec, gb_spec, mask_spec, map_spec, map_spec] + quarters,
        (map_b, map_f, shape((2, channels)), shape2, gw_shape, gw_shape),
        (map_spec, map_spec, whole((2, channels)), spec2, own_spec, other_spec),
        [
            pltpu.VMEM((pixels_here, channels), BF16),
            pltpu.VMEM((channels, pixels_here), BF16),
            pltpu.VMEM((channels, pixels_here), BF16),
            pltpu.VMEM((pixels_here, channels), F32),
            pltpu.VMEM((pixels_here, channels), F32),
            pltpu.VMEM((2, channels), F32),
            pltpu.VMEM((channels, 2 * wide), BF16),
            pltpu.VMEM((channels, 2 * wide), BF16),
        ],
    )
    st, output, gn, gown, gother, back_normal = tie(st, output, gn, gown, gother, back_normal)
    gffn = by_bits(added(gown, swapped(gother)).reshape(count // 2, -1, 2 * hidden_here))
    left = list(reversed(range(bits)))
    kept_a, sent_a = split_bit(gffn[..., :hidden_here], left, 0)
    kept_b, sent_b = split_bit(gffn[..., hidden_here:], left, 1)
    st, kept_a, sent_a, kept_b, sent_b = tie(exchange(st), kept_a, sent_a, kept_b, sent_b)
    sent_a, sent_b = send_bit(sent_a, 0), send_bit(sent_b, 1)

    gw_here = shape((channels, channels), BF16)
    gblock, gout, g, sums_four, st = call(
        11,
        functools.partial(merge_back_kernel, STEPS),
        (STEPS,),
        (st, norm, norm_two, norm_four, gb, mask, block, gn, ct, merged, large, small, w_out),
        [spec2, norm_spec, whole((4, channels)), whole((2, channels)), gb_spec, row_1] + [row_c] * 6 + [square],
        (map_f, gw_here, map_f, shape((2, channels)), shape3),
        (row_c, square, row_c, whole((2, channels)), spec3),
        [pltpu.VMEM((2, channels), F32), pltpu.VMEM((3, channels), F32), pltpu.VMEM((channels, channels), F32)],
    )
    st, gblock, gout, g, sent_a, sent_b = tie(st, gblock, gout, g, sent_a, sent_b)
    kept_a, sent_a = split_bit(added(kept_a, sent_a), left[:-1], 1)
    kept_b, sent_b = split_bit(added(kept_b, sent_b), left[:-2] + [0], 0)
    st, gout, kept_a, sent_a, kept_b, sent_b = tie(exchange(st), gout, kept_a, sent_a, kept_b, sent_b)
    sent_a, sent_b = send_bit(sent_a, 1), send_bit(sent_b, 0)
    gout = exchange(gout.reshape(count, share, channels))

    gk_shape = shape((channels, large_wide + small_wide), BF16)
    map_chunk = chunk_rows(pixels_here)
    g, gk, sums_two, st = call(
        21,
        functools.partial(spread_back_kernel, images),
        (chunks,),
        (st, norm, norm_one, norm_two, gb, mask, inner, large, small, g, moved, fourier, back, tap_large, tap_small, waves_large, waves_small),
        [chunk_stats(3), chunk_rows(3), chunk_rows(2), chunk_rows(4), chunk_rows(16), mask_spec, map_chunk, map_chunk, map_chunk, map_chunk,
         moved_spec, four_spec, back_spec, tap_spec, tap_spec, wl_spec, ws_spec],
        (map_f, gk_shape, shape((3, channels)), shape2),
        (map_chunk, kt_spec, chunk_rows(3), chunk_stats(2)),
    )
    st, gk, g, gout, sent_a, sent_b = tie(st, gk, g, gout, sent_a, sent_b)
    kept, sent = split_hid(gk)
    gk = added(kept, swapped(sent))
    gffn = jnp.concatenate([added(kept_a, sent_a), added(kept_b, sent_b)], axis=-1)
    kept_f, sent_f = split_bit(gffn, left[:-2], left[0])
    st, gk, kept_f, sent_f = tie(exchange(st), gk, kept_f, sent_f)
    gk = to_chips(gk)
    sent_f = send_bit(sent_f, left[0])

    all_images = whole((images, SPOTS, channels))

    def as_images(array):
        return array.reshape(images, SPOTS, channels)

    own, prev, gin, sums_one, st = call(
        12,
        functools.partial(unmix_kernel, images),
        (images,),
        (
            relative, ratios, st, norm, norm_one, gb, mask, as_images(inner), as_images(g), as_images(first),
            as_images(gblock), as_images(x), w_in, target_row,
        ),
        [spec2, norm_spec, whole((2, channels)), gb_spec, image_mask] + [image_spec] * 5 + [square, row_spec],
        (
            image_f, shape((images, SPOTS, channels), BF16), gw_here, shape((2, channels)),
            shape((count, 6, channels), BF16),
        ),
        (all_images, all_images, square, whole((2, channels)), whole((count, 6, channels))),
        [
            pltpu.VMEM((images, SPOTS, channels), F32),
            pltpu.VMEM((2, channels), F32),
            pltpu.VMEM((2, channels), F32),
            pltpu.VMEM((channels, channels), F32),
        ],
        prefetch=2,
    )
    st, own, prev, gin, sent_f = tie(st, own, prev, gin, sent_f)
    returned = shifted(prev, -1)
    gffn = added(kept_f, sent_f, F32 if bits == 3 else BF16)
    for bit in left[1:-2]:
        kept, sent = split_bit(gffn, left[left.index(bit) : -2], bit)
        gffn = added(kept, send_bit(sent, bit), BF16 if bit > 2 else F32)
    gin = jnp.concatenate([gin.reshape(count, share, channels), st], axis=1)
    gin = exchange(gin).astype(F32)
    st = jnp.sum(gin[:, share:], axis=0)
    st = (st[0:2] + st[2:4] + st[4:6])[None]
    gin, gk, gout = (jnp.sum(part.astype(F32), axis=0) for part in (gin[:, :share], gk, gout))
    broad_spec = pl.BlockSpec((1,) + broad[1:], lambda i: (i, 0, 0))
    one_image = pl.BlockSpec((1, SPOTS, channels), lambda i: (i, 0, 0))
    (given,) = call(
        100, returned_kernel, (images,), (own, returned), [one_image, one_image], (image_f,), (one_image,)
    )
    grad_raw, sums_zero = call(
        4,
        finish_kernel,
        (images,),
        (st, norm, gb, given, own_normal, back_normal),
        [whole((1, 2, channels)), norm_spec, gb_spec, one_image, broad_spec, broad_spec],
        (image_f, shape((2, channels))),
        (one_image, whole((2, channels))),
    )

    gains = jnp.concatenate([sums_zero[1:2], sums_one[1:2], sums_two[1:3], sums_four[1:2]], axis=0)
    biases = jnp.concatenate([sums_zero[0:1], sums_one[0:1], sums_two[0:1], sums_two[0:1], sums_four[0:1]], axis=0)
    gffn = gffn.reshape(-1, per_half, 2, wide)
    canvas = (images, CANVAS, CANVAS, channels)
    return (
        output.reshape(canvas),
        grad_raw.reshape(canvas),
        gin,
        gk[:, :large_taps].T.reshape(large_extent, large_extent, share),
        gk[:, large_wide : large_wide + small_taps].T.reshape(small_extent, small_extent, share),
        gout,
        lax.dynamic_slice_in_dim(gains, position * share, share, 1),
        lax.dynamic_slice_in_dim(biases, position * share, share, 1),
        gffn[:, :, 0].reshape(-1, hidden_here),
        gffn[:, :, 1].reshape(-1, hidden_here).T,
    )


def solution(mesh):
    one = P(BOTH)
    maps = P(BOTH, None, None, None)
    flat = P(BOTH, None)
    kernels = P(None, None, BOTH)
    norms = P(None, BOTH)
    return jax.shard_map(
        shards,
        mesh=mesh,
        in_specs=(
            maps, one, one, flat, one, one, flat, kernels, kernels, flat, norms, norms,
            P("batch", "hid"), P("hid", "batch"), maps,
        ),
        out_specs=(maps, maps, flat, kernels, kernels, flat, norms, norms, P("batch", "hid"), P("hid", "batch")),
        check_vma=False,
    )
```
